256 devices in a mesh: tm: 8 (over z), traj: 32 (over y, x, core).
Axes of the slice: x: 4, y: 4, z: 8, core: 2. Of those that a mesh axis runs over, the one named last changes fastest.
Arguments:
- states: bfloat16 [32, 2048, 1024], P('traj', 'tm'), may hold values from -6 to 6
- episode_end: int32 [32, 2048], P('traj', 'tm'), may hold values 0 or 1
- feature_head: bfloat16 [1024, 128], replicated, may hold values from -0.1875 to 0.1875
- successor_head: bfloat16 [1024, 2048], replicated, may hold values from -0.1875 to 0.1875
- horizon_gap: float32 [16], replicated, may hold values from 1e-05 to 0.01
- trace_gap: float32 [16], replicated, may hold values from 1e-05 to 0.03
Outputs:
- returns: bfloat16 [32, 2048, 2048], P('traj', 'tm')
- head_grad: float32 [1024, 2048], P('traj', 'tm')
The draws below stay inside these ranges and needn't reach their ends.
All inputs are finite; a program needn't handle non-finite values. No bound on the sum of `episode_end` on one device may be relied on, other than what follows from the above.
Results may differ from the reference program's by a relative error of at most 0.0095.
Values may be sent and summed in bfloat16 or wider, within the bound.
No kernel may reach another device: no remote copies, remote signals or barrier semaphores. Data moves between devices by JAX's collectives and lax.ppermute only.
A program may use at most 64 MiB of HBM per device.

```python
import math
import jax
import jax.numpy as jnp
from jax import lax

E = 1024
F = 128
K = 16
KF = 2048
STEPS = 2048
TRAJ = 32


def place_ends(array, stream_key, low, top_value):
    place = [jax.random.randint(jax.random.fold_in(stream_key, axis), (), 0, length) for axis, length in enumerate(array.shape)]
    longest = array.shape.index(max(array.shape))
    next_to = place[:longest] + [(place[longest] + 1) % array.shape[longest]] + place[longest + 1:]
    return array.at[tuple(place)].set(low).at[tuple(next_to)].set(top_value)


def level_of(rng, dims, split, smallest, top_value):
    level, own = 1.0, jax.random.fold_in(rng, 6)
    for axis_at, blocks in split:
        draws = jnp.exp(jax.random.uniform(jax.random.fold_in(own, axis_at), (blocks,), jnp.float32, smallest / len(split), top_value / len(split)))
        level = level * jnp.repeat(draws, dims[axis_at] // blocks).reshape([-1 if axis == axis_at else 1 for axis in range(len(dims))])
    return level


def normal_values(stream_key, shape, deviation, limit, cuts=(), held_as=jnp.bfloat16):
    array = deviation * jax.random.normal(stream_key, shape, jnp.float32)
    if cuts:
        array = array * level_of(stream_key, shape, cuts, -0.22, 0.18)
    return jnp.clip(array, -limit, limit).astype(held_as)


def setup_inputs(seed: int = 0) -> dict:
    seeds = jax.random.split(jax.random.key(seed), 7)
    return {
        "states": normal_values(seeds[0], (TRAJ, STEPS, E), 1.0, 6.0, ((0, 32), (1, 8))),
        "episode_end": place_ends((jax.random.randint(seeds[1], (TRAJ, STEPS), 0, 2 * STEPS) < 1).astype(jnp.int32), jax.random.fold_in(seeds[1], 1), 0, 1),
        "feature_head": normal_values(seeds[2], (E, F), E ** -0.5, 0.1875),
        "successor_head": normal_values(seeds[3], (E, KF), E ** -0.5, 0.1875),
        "horizon_gap": jnp.clip(jnp.exp(jax.random.uniform(seeds[4], (K,), jnp.float32, math.log(9.999999747378752e-06), math.log(0.01))), 9.999999747378752e-06, 0.01),
        "trace_gap": jnp.clip(jnp.exp(jax.random.uniform(seeds[5], (K,), jnp.float32, math.log(9.999999747378752e-06), math.log(0.03))), 9.999999747378752e-06, 0.03),
    }


def reference(states, episode_end, feature_head, successor_head, horizon_gap, trace_gap):
    discount = 1.0 - horizon_gap
    rate = discount * (1.0 - trace_gap)
    scale_k = jnp.sqrt(1.0 - rate * rate)
    boot = discount * trace_gap

    def heads(state_rows):
        feats = jnp.dot(state_rows, feature_head, preferred_element_type=jnp.float32)
        preds = jnp.dot(state_rows, successor_head, preferred_element_type=jnp.float32).astype(jnp.bfloat16)
        return (feats, preds)
    features, pred = lax.map(heads, states)
    pred_next = jnp.concatenate([pred[:, 1:], jnp.zeros_like(pred[:, :1])], axis=1)
    keep = 1.0 - episode_end.astype(jnp.float32)

    def step(carry, inputs):
        feat_t, next_t, keep_t = inputs
        next_f = next_t.astype(jnp.float32).reshape(next_t.shape[0], K, F)
        source = scale_k[None, :, None] * feat_t[:, None, :] + boot[None, :, None] * keep_t[:, None, None] * next_f
        value = source + rate[None, :, None] * keep_t[:, None, None] * carry
        return (value, value)
    init = jnp.zeros((TRAJ, K, F), jnp.float32)
    xs = (jnp.swapaxes(features, 0, 1), jnp.swapaxes(pred_next, 0, 1), jnp.swapaxes(keep, 0, 1))
    last, values = lax.scan(step, init, xs, reverse=True)
    values = jnp.swapaxes(values, 0, 1).reshape(TRAJ, STEPS, KF)
    returns = values.astype(jnp.bfloat16)
    resid = (pred.astype(jnp.float32) - values).astype(jnp.bfloat16)

    def accum(total, pair):
        rows, errs = pair
        part = lax.dot_general(rows, errs, (((0,), (0,)), ((), ())), preferred_element_type=jnp.float32)
        return (total + part, None)
    total, unused = lax.scan(accum, jnp.zeros((E, KF), jnp.float32), (states, resid))
    head_grad = total / jnp.sqrt(jnp.float32(TRAJ * STEPS))
    return (returns, head_grad)
```

```python
import functools
import jax
import jax.numpy as jnp
from jax import lax
from jax.experimental import pallas as pl
from jax.experimental.pallas import tpu as pltpu
from jax.sharding import Mesh, PartitionSpec as P

F = 128
MIB = 1 << 20
f32, bf16 = jnp.float32, jnp.bfloat16
SMEM = pl.BlockSpec(memory_space=pltpu.SMEM)


def coefficients(hg_ref, tg_ref, k):
    hg = jnp.full((1, F), hg_ref[k], f32)
    tg = jnp.full((1, F), tg_ref[k], f32)
    discount = 1.0 - hg
    rate = discount * (1.0 - tg)
    return jnp.log(rate), jnp.sqrt(1.0 - rate * rate), discount * tg / rate


def iota(shape, dim):
    return lax.broadcasted_iota(jnp.int32, shape, dim)


def local_kernel(hg_ref, tg_ref, end_ref, s_ref, wf_ref, w_ref, p_ref, g_ref, msg_ref, open_ref, f_ref, mask_ref):
    i = pl.program_id(0)
    steps = s_ref.shape[0]
    per = w_ref.shape[1] // F
    num_k = hg_ref.shape[0]

    @pl.when(i == 0)
    def _():
        f_ref[...] = jnp.dot(s_ref[...], wf_ref[...], preferred_element_type=f32)
        rows, cols = iota((steps, steps), 0), iota((steps, steps), 1)
        ended = jnp.broadcast_to(end_ref[...].astype(f32), (steps, steps)).astype(bf16)
        below = (cols < rows).astype(f32).astype(bf16)
        above = (rows < cols).astype(f32).astype(bf16)
        at_row = lax.dot_general(below, ended, (((1,), (1,)), ((), ())), preferred_element_type=f32)
        at_col = jnp.dot(ended, above, preferred_element_type=f32)
        mask_ref[...] = jnp.where((at_row == at_col) & (cols >= rows), 1.0, 0.0).astype(bf16)
        total = jnp.sum(end_ref[...].astype(f32), axis=1, keepdims=True)
        open_ref[...] = jnp.where(at_row[:, :F] == total, 1.0, 0.0)
        for z in range(msg_ref.shape[0]):
            msg_ref[z, num_k:, :] = jnp.broadcast_to(jnp.where(total == 0.0, 1.0, 0.0), (msg_ref.shape[1] - num_k, F))

    pred = jnp.dot(s_ref[...], w_ref[...], preferred_element_type=f32).astype(bf16)
    p_ref[...] = pred
    t = iota((steps, F), 0).astype(f32)
    scaled, backs, betas = [], [], []
    for j in range(per):
        log_rate, scale, beta = coefficients(hg_ref, tg_ref, i * per + j)
        q = scale * f_ref[...] + beta * pred[:, j * F : (j + 1) * F].astype(f32)
        scaled.append(jnp.exp(t * log_rate) * q)
        backs.append(jnp.exp(-t * log_rate))
        betas.append(beta)
    scaled = jnp.concatenate(scaled, axis=1)
    high = scaled.astype(bf16)
    low = (scaled - high.astype(f32)).astype(bf16)
    sums = jnp.dot(mask_ref[...], high, preferred_element_type=f32)
    sums = sums + jnp.dot(mask_ref[...], low, preferred_element_type=f32)
    for j in range(per):
        cols = slice(j * F, (j + 1) * F)
        h = backs[j] * sums[:, cols]
        g_ref[:, cols] = h - betas[j] * pred[:, cols].astype(f32)
        for z in range(msg_ref.shape[0]):
            msg_ref[z, pl.ds(i * per + j, 1), :] = h[:1]


def finish_kernel(axis, hg_ref, tg_ref, msg_ref, open_ref, p_ref, g_ref, ret_ref, res_ref):
    i = pl.program_id(0)
    here = lax.axis_index(axis)
    steps = p_ref.shape[0]
    per = p_ref.shape[1] // F
    num_k = hg_ref.shape[0]
    t = iota((steps, F), 0).astype(f32)
    for j in range(per):
        k = i * per + j
        log_rate, _, _ = coefficients(hg_ref, tg_ref, k)
        through = jnp.exp(steps * log_rate)
        later = jnp.zeros((1, F), f32)
        for z in range(msg_ref.shape[0] - 1, 0, -1):
            block = msg_ref[z, pl.ds(k, 1), :] + through * msg_ref[z, num_k : num_k + 1, :] * later
            later = jnp.where(z > here, block, later)
        cols = slice(j * F, (j + 1) * F)
        g = g_ref[:, cols] + open_ref[...] * jnp.exp((steps - t) * log_rate) * later
        ret_ref[:, cols] = g.astype(bf16)
        res_ref[:, cols] = (p_ref[:, cols].astype(f32) - g).astype(bf16)


def grad_kernel(axis, s_ref, so_ref, r_ref, ro_ref, g_ref, st_ref, sto_ref):
    parts, rows, _ = g_ref.shape
    width = s_ref.shape[1]

    @pl.when(pl.program_id(0) == 0)
    def _():
        c = lax.axis_index(axis)
        r = iota((parts * rows, width), 0)
        want = (r // rows) * (2 * rows) + c * rows + r % rows
        pick = (want == iota((parts * rows, width), 1)).astype(f32).astype(bf16)
        contract = (((1,), (1,)), ((), ()))
        st_ref[...] = lax.dot_general(pick, s_ref[...], contract, preferred_element_type=f32).astype(bf16)
        sto_ref[...] = lax.dot_general(pick, so_ref[...], contract, preferred_element_type=f32).astype(bf16)

    g = jnp.dot(st_ref[...], r_ref[...], preferred_element_type=f32)
    g = g + jnp.dot(sto_ref[...], ro_ref[...], preferred_element_type=f32)
    g_ref[...] = g.astype(bf16).reshape(g_ref.shape)


def sum_kernel(x_ref, y_ref):
    y_ref[0] = jnp.sum(x_ref[...].astype(f32), axis=0).astype(y_ref.dtype)


def final_kernel(norm, x_ref, y_ref):
    y_ref[...] = jnp.sum(x_ref[...].astype(f32), axis=0) * norm


def params(mib=40):
    return pltpu.CompilerParams(vmem_limit_bytes=mib * MIB)


def whole(shape):
    return pl.BlockSpec(shape, lambda i: (0,) * len(shape))


def columns(rows, width):
    return pl.BlockSpec((rows, width), lambda i: (0, i))


def body(states, episode_end, feature_head, successor_head, horizon_gap, trace_gap):
    steps, width = states.shape[1:]
    num_k = horizon_gap.shape[0]
    kf = successor_head.shape[1]
    nz, ny, nx, nc = (lax.axis_size(a) for a in ("z", "y", "x", "c"))
    s = states[0]
    swap = [(a, nc - 1 - a) for a in range(nc)]
    s_other = lax.ppermute(s, "c", swap)
    blk = 2 * F
    n = kf // blk
    msg_rows = num_k + 8
    pred, g_local, msg, still_open = pl.pallas_call(
        local_kernel,
        grid=(n,),
        in_specs=[SMEM, SMEM, whole((1, steps)), whole((steps, width)), whole((width, F)), columns(width, blk)],
        out_specs=[columns(steps, blk), columns(steps, blk), whole((nz, msg_rows, F)), whole((steps, F))],
        out_shape=[
            jax.ShapeDtypeStruct((steps, kf), bf16),
            jax.ShapeDtypeStruct((steps, kf), f32),
            jax.ShapeDtypeStruct((nz, msg_rows, F), f32),
            jax.ShapeDtypeStruct((steps, F), f32),
        ],
        scratch_shapes=[pltpu.VMEM((steps, F), f32), pltpu.VMEM((steps, steps), bf16)],
        compiler_params=params(),
        name="local",
    )(horizon_gap, trace_gap, episode_end, s, feature_head, successor_head)
    msg = lax.all_to_all(msg, "z", 0, 0, tiled=True)
    returns, resid = pl.pallas_call(
        functools.partial(finish_kernel, "z"),
        grid=(n,),
        in_specs=[SMEM, SMEM, whole((nz, msg_rows, F)), whole((steps, F)), columns(steps, blk), columns(steps, blk)],
        out_specs=[columns(steps, blk), columns(steps, blk)],
        out_shape=[jax.ShapeDtypeStruct((steps, kf), bf16)] * 2,
        compiler_params=params(),
        name="finish",
    )(horizon_gap, trace_gap, msg, still_open, pred, g_local)
    resid_other = lax.ppermute(resid, "c", swap)
    parts, rows = ny * nx, width // (ny * nx * nc)
    gblk = 4 * F
    grad = pl.pallas_call(
        functools.partial(grad_kernel, "c"),
        grid=(kf // gblk,),
        in_specs=[whole((steps, width)), whole((steps, width)), columns(steps, gblk), columns(steps, gblk)],
        out_specs=pl.BlockSpec((parts, rows, gblk), lambda i: (0, 0, i)),
        out_shape=jax.ShapeDtypeStruct((parts, rows, kf), bf16),
        scratch_shapes=[pltpu.VMEM((parts * rows, steps), bf16)] * 2,
        compiler_params=params(),
        name="grad",
    )(s, s_other, resid, resid_other)
    grad = lax.all_to_all(grad, ("y", "x"), 0, 0, tiled=True)
    cols = kf // nz
    grad = pl.pallas_call(
        sum_kernel,
        grid=(nz,),
        in_specs=[pl.BlockSpec((parts, rows, cols), lambda i: (0, 0, i))],
        out_specs=pl.BlockSpec((1, rows, cols), lambda i: (i, 0, 0)),
        out_shape=jax.ShapeDtypeStruct((nz, rows, cols), bf16),
        compiler_params=params(),
        name="sum_plane",
    )(grad)
    grad = lax.all_to_all(grad, "z", 0, 0, tiled=True)
    norm = float(steps * nz * ny * nx * nc) ** -0.5
    head_grad = pl.pallas_call(
        functools.partial(final_kernel, norm),
        out_shape=jax.ShapeDtypeStruct((rows, cols), f32),
        name="sum_line",
    )(grad)
    return returns[None], head_grad


def solution(mesh):
    grid = Mesh(mesh.devices.reshape(8, 4, 4, 2), ("z", "y", "x", "c"))
    traj = ("y", "x", "c")
    return jax.shard_map(
        body,
        mesh=grid,
        in_specs=(P(traj, "z", None), P(traj, "z"), P(), P(), P(), P()),
        out_specs=(P(traj, "z", None), P(traj, "z")),
        check_vma=False,
    )
```

```python
import functools
import itertools
import jax
import jax.numpy as jnp
from jax import lax
from jax.experimental import pallas as pl
from jax.experimental.pallas import tpu as pltpu
from jax.sharding import Mesh, PartitionSpec as P

F = 128
MIB = 1 << 20
TAIL = 16
AXES = ("z", "y", "x", "c")
SIZES = (8, 4, 4, 2)
f32, bf16 = jnp.float32, jnp.bfloat16
SMEM = pl.BlockSpec(memory_space=pltpu.SMEM)
VMEM = pl.BlockSpec(memory_space=pltpu.VMEM)
HBM = pl.BlockSpec(memory_space=pltpu.HBM)
OFFSETS = list(itertools.product((0, 1), repeat=3))


def iota(shape, dim):
    return lax.broadcasted_iota(jnp.int32, shape, dim)


def coefficients(hg_ref, tg_ref, k):
    hg = jnp.full((1, F), hg_ref[k], f32)
    tg = jnp.full((1, F), tg_ref[k], f32)
    discount = 1.0 - hg
    rate = discount * (1.0 - tg)
    return jnp.log(rate), jnp.sqrt(1.0 - rate * rate), discount * tg / rate


def powers(log_rate, steps):
    a = jnp.exp(iota((steps // 8, F), 0).astype(f32) * (8.0 * log_rate))
    b = jnp.exp(iota((8, F), 0).astype(f32) * log_rate)
    return (a[:, None, :] * b[None, :, :]).reshape(steps, F)


def ends_before(ended_row, steps):
    ended = jnp.broadcast_to(ended_row, (F, steps)).astype(bf16)
    below = (iota((steps, steps), 1) < iota((steps, steps), 0)).astype(f32).astype(bf16)
    return lax.dot_general(below, ended, (((1,), (1,)), ((), ())), preferred_element_type=f32)


def open_rows(ended_row, steps):
    total = jnp.sum(ended_row, axis=1, keepdims=True)
    return jnp.where(ends_before(ended_row, steps) == total, 1.0, 0.0)


def local_kernel(hg_hbm, tg_hbm, end_hbm, s_hbm, wf_hbm, w_hbm, r_ref, g_ref, msg_ref, thru_ref, open_ref,
                 hg_ref, tg_ref, end_ref, s_ref, wf_ref, w_ref, sems):
    blocks, _, blk = w_ref.shape
    steps = s_ref.shape[0]
    num_k = hg_ref.shape[0]
    copies = [
        pltpu.make_async_copy(a, b, sems.at[n])
        for n, (a, b) in enumerate(
            [(hg_hbm, hg_ref), (tg_hbm, tg_ref), (end_hbm, end_ref), (s_hbm, s_ref), (wf_hbm, wf_ref)]
            + [(w_hbm.at[:, i * blk : (i + 1) * blk], w_ref.at[i]) for i in range(blocks)]
        )
    ]
    for copy in copies:
        copy.start()
    for copy in copies[:3]:
        copy.wait()
    ended_row = end_ref[...].astype(f32)
    rows, cols = iota((steps, steps), 0), iota((steps, steps), 1)
    at_row = ends_before(ended_row, steps)
    ended = jnp.broadcast_to(ended_row, (steps, steps)).astype(bf16)
    above = (rows < cols).astype(f32).astype(bf16)
    at_col = jnp.dot(ended, above, preferred_element_type=f32)
    at_rows = jnp.concatenate([at_row] * (steps // F), axis=1)
    mask = jnp.where((at_rows == at_col) & (cols >= rows), 1.0, 0.0).astype(bf16)
    total = jnp.sum(ended_row, axis=1, keepdims=True)
    open_ref[...] = jnp.where(at_row == total, 1.0, 0.0)
    for z in range(msg_ref.shape[0]):
        msg_ref[z, num_k:, :] = jnp.broadcast_to(jnp.where(total == 0.0, 1.0, 0.0), (msg_ref.shape[1] - num_k, F))
    r_ref[steps:, :] = jnp.zeros((TAIL, r_ref.shape[1]), bf16)
    r_ref[steps:, :steps] = jnp.broadcast_to(ended_row, (TAIL, steps)).astype(bf16)

    for copy in copies[3:5]:
        copy.wait()
    s = s_ref[...]
    f = jnp.dot(s, wf_ref[...], preferred_element_type=f32)
    for i in range(blocks):
        copies[5 + i].wait()
        pred = jnp.dot(s, w_ref[i], preferred_element_type=f32).astype(bf16)
        scaled, backs, biased = [], [], []
        for j in range(blk // F):
            log_rate, scale, beta = coefficients(hg_ref, tg_ref, i * (blk // F) + j)
            thru_ref[i * (blk // F) + j : i * (blk // F) + j + 1, :] = jnp.exp(steps * log_rate)
            p = pred[:, j * F : (j + 1) * F].astype(f32)
            biased.append((p, beta * p))
            scaled.append(powers(log_rate, steps) * (scale * f + biased[j][1]))
            backs.append(powers(-log_rate, steps))
        scaled = jnp.concatenate(scaled, axis=1)
        high = scaled.astype(bf16)
        low = (scaled - high.astype(f32)).astype(bf16)
        sums = jnp.dot(mask, high, preferred_element_type=f32)
        sums = sums + jnp.dot(mask, low, preferred_element_type=f32)
        for j in range(blk // F):
            k = i * (blk // F) + j
            cols = slice(k * F, (k + 1) * F)
            h = backs[j] * sums[:, j * F : (j + 1) * F]
            g = h - biased[j][1]
            g_ref[:, cols] = g
            r_ref[:steps, cols] = (biased[j][0] - g).astype(bf16)
            for z in range(msg_ref.shape[0]):
                msg_ref[z, k : k + 1, :] = h[:1]


def later_kernel(msg_ref, thru_ref, h_ref):
    here = lax.axis_index("z")
    num_k = thru_ref.shape[0]
    later = jnp.zeros((num_k, F), f32)
    for z in range(msg_ref.shape[0] - 1, 0, -1):
        block = msg_ref[z, :num_k, :] + thru_ref[...] * msg_ref[z, num_k : num_k + 1, :] * later
        later = jnp.where(z > here, block, later)
    h_ref[...] = later


def backwards(log_rate, steps):
    return jnp.exp(steps * log_rate) * powers(-log_rate, steps)


def returns_kernel(hg_ref, tg_ref, h_ref, open_ref, g_ref, out_ref):
    steps = g_ref.shape[0]
    still = open_ref[...]
    for k in range(hg_ref.shape[0]):
        cols = slice(k * F, (k + 1) * F)
        decay = still * backwards(coefficients(hg_ref, tg_ref, k)[0], steps)
        out_ref[:, cols] = (g_ref[:, cols] + decay * h_ref[k : k + 1, :]).astype(bf16)


def grad_kernel(dz, hg_ref, tg_ref, s_ref, so_ref, r_ref, ro_ref, h_ref, ho_ref, open_ref, *outs):
    steps, width = s_ref.shape
    halves, quads, rows, cols = outs[0].shape
    num_k = h_ref.shape[0]
    per = cols // F
    z, y, x, c = (lax.axis_index(a) for a in AXES)
    py, px, pz = y % 2, x % 2, (z + dz) % 2
    tall = len(outs) * quads * rows
    r = iota((tall, 1), 0)
    part, quad = r // (quads * rows), (r // rows) % quads
    row_y = 2 * (quad // 2) + (part // 2 + py) % 2
    row_x = 2 * (quad % 2) + (part % 2 + px) % 2
    want = ((row_y * SIZES[2] + row_x) * SIZES[3] + c) * rows + r % rows
    pick = (want == iota((tall, width), 1)).astype(f32).astype(bf16)
    contract = (((1,), (1,)), ((), ()))
    st = lax.dot_general(pick, s_ref[...], contract, preferred_element_type=f32).astype(bf16)
    sto = lax.dot_general(pick, so_ref[...], contract, preferred_element_type=f32).astype(bf16)
    still = open_ref[...]
    still_o = open_rows(ro_ref[steps : steps + 1, :steps].astype(f32), steps)
    for half in range(halves):
        first = (2 * half + pz) * per
        mine, other = [], []
        for j in range(per):
            k = first + j
            at = pl.ds(pl.multiple_of(k * F, F), F)
            back = backwards(coefficients(hg_ref, tg_ref, k)[0], steps)
            mine.append((r_ref[:steps, at].astype(f32) - still * back * h_ref[pl.ds(k, 1), :]).astype(bf16))
            other.append((ro_ref[:steps, at].astype(f32) - still_o * back * ho_ref[pl.ds(k, 1), :]).astype(bf16))
        g = jnp.dot(st, jnp.concatenate(mine, axis=1), preferred_element_type=f32)
        g = g + jnp.dot(sto, jnp.concatenate(other, axis=1), preferred_element_type=f32)
        g = g.astype(bf16).reshape(len(outs), quads, rows, cols)
        for n, out in enumerate(outs):
            out[half] = g[n]


def cube_kernel(*refs):
    *ins, out_ref = refs
    for half in range(out_ref.shape[0]):
        total = ins[0][half].astype(f32)
        for ref in ins[1:]:
            total = total + ref[half].astype(f32)
        out_ref[half] = total.astype(out_ref.dtype)


def final_kernel(norm, x_ref, y_ref):
    y_ref[...] = jnp.sum(x_ref[...].astype(f32), axis=0) * norm


def params(mib=48):
    return pltpu.CompilerParams(vmem_limit_bytes=mib * MIB)


def flat(place):
    n = 0
    for i, size in zip(place, SIZES):
        n = n * size + i
    return n


def across(offset):
    pairs = []
    for place in itertools.product(*(range(n) for n in SIZES)):
        core = place[3]
        to = [
            i if not d else (i ^ 1 if core == 0 else ((i + 1) % n if i % 2 else (i - 1) % n))
            for i, d, n in zip(place, offset, SIZES)
        ]
        pairs.append((flat(place), flat(to + [core])))
    return pairs


def alike():
    return [
        [flat((2 * z + pz, 2 * y + py, 2 * x + px, c)) for z in range(4) for y in range(2) for x in range(2)]
        for c in range(2)
        for pz, py, px in OFFSETS
    ]


def body(states, episode_end, feature_head, successor_head, horizon_gap, trace_gap):
    steps, width = states.shape[1:]
    num_k = horizon_gap.shape[0]
    kf = successor_head.shape[1]
    nz, ny, nx, nc = SIZES
    s = states[0]
    swap = [(0, 1), (1, 0)]
    s_other = lax.ppermute(s, "c", swap)
    blk = 4 * F
    n = kf // blk
    shape = jax.ShapeDtypeStruct
    resid, g_local, msg, thru, still_open = pl.pallas_call(
        local_kernel,
        in_specs=[HBM] * 6,
        out_specs=[VMEM] * 5,
        out_shape=[
            shape((steps + TAIL, kf), bf16),
            shape((steps, kf), f32),
            shape((nz, num_k + 8, F), f32),
            shape((num_k, F), f32),
            shape((steps, F), f32),
        ],
        scratch_shapes=[
            pltpu.SMEM((num_k,), f32),
            pltpu.SMEM((num_k,), f32),
            pltpu.VMEM((1, steps), jnp.int32),
            pltpu.VMEM((steps, width), bf16),
            pltpu.VMEM((width, F), bf16),
            pltpu.VMEM((n, width, blk), bf16),
            pltpu.SemaphoreType.DMA((5 + n,)),
        ],
        compiler_params=params(),
        name="local",
    )(horizon_gap, trace_gap, episode_end, s, feature_head, successor_head)
    resid_other = lax.ppermute(resid, "c", swap)
    msg = lax.all_to_all(msg, "z", 0, 0, tiled=True)
    later = pl.pallas_call(
        later_kernel,
        in_specs=[VMEM] * 2,
        out_specs=VMEM,
        out_shape=shape((num_k, F), f32),
        name="later",
    )(msg, thru)
    later_other = lax.ppermute(later, "c", swap)
    rows, cols = width // (ny * nx * nc), kf // nz
    chunk = (nz // 2, ny * nx // 4, rows, cols)

    def grads(dz):
        return pl.pallas_call(
            functools.partial(grad_kernel, dz),
            in_specs=[SMEM] * 2 + [VMEM] * 7,
            out_specs=[VMEM] * 4,
            out_shape=[shape(chunk, bf16)] * 4,
            compiler_params=params(),
            name="grad",
        )(horizon_gap, trace_gap, s, s_other, resid, resid_other, later, later_other, still_open)

    chunks = dict(zip([o for o in OFFSETS if o[0] == 1], grads(1)))
    chunks |= dict(zip([o for o in OFFSETS if o[0] == 0], grads(0)))
    sums = [chunks[0, 0, 0]] + [lax.ppermute(chunks[o], AXES, across(o)) for o in reversed(OFFSETS[1:])]
    returns = pl.pallas_call(
        returns_kernel,
        in_specs=[SMEM] * 2 + [VMEM] * 3,
        out_specs=VMEM,
        out_shape=shape((steps, kf), bf16),
        compiler_params=params(),
        name="returns",
    )(horizon_gap, trace_gap, later, still_open, g_local)
    grad = pl.pallas_call(
        cube_kernel,
        in_specs=[VMEM] * 8,
        out_specs=VMEM,
        out_shape=shape(chunk, bf16),
        compiler_params=params(),
        name="sum_cube",
    )(*sums)
    grad = lax.all_to_all(grad.reshape(-1, rows, cols), AXES, 0, 0, axis_index_groups=alike())
    norm = float(steps * nz * ny * nx * nc) ** -0.5
    head_grad = pl.pallas_call(
        functools.partial(final_kernel, norm),
        in_specs=[VMEM],
        out_specs=VMEM,
        out_shape=shape((rows, cols), f32),
        name="sum_rest",
    )(grad)
    return returns[None], head_grad


def solution(mesh):
    grid = Mesh(mesh.devices.reshape(SIZES), AXES)
    traj = ("y", "x", "c")
    return jax.shard_map(
        body,
        mesh=grid,
        in_specs=(P(traj, "z", None), P(traj, "z"), P(), P(), P(), P()),
        out_specs=(P(traj, "z", None), P(traj, "z")),
        check_vma=False,
    )
```

```python
import functools
import itertools
import jax
import jax.numpy as jnp
from jax import lax
from jax.experimental import pallas as pl
from jax.experimental.pallas import tpu as pltpu
from jax.sharding import Mesh, PartitionSpec as P

F = 128
MIB = 1 << 20
AXES = ("z", "y", "x", "c")
SIZES = (8, 4, 4, 2)
f32, bf16 = jnp.float32, jnp.bfloat16
SMEM = pl.BlockSpec(memory_space=pltpu.SMEM)
VMEM = pl.BlockSpec(memory_space=pltpu.VMEM)
HBM = pl.BlockSpec(memory_space=pltpu.HBM)
OFFSETS = list(itertools.product((0, 1), repeat=3))
ORDER = [(1, 0, 0), (0, 1, 0), (0, 0, 1), (1, 1, 1), (1, 1, 0), (1, 0, 1), (0, 1, 1)]


def iota(shape, dim):
    return lax.broadcasted_iota(jnp.int32, shape, dim)


def coefficients(hg_ref, tg_ref, k):
    hg = jnp.full((1, F), hg_ref[k], f32)
    tg = jnp.full((1, F), tg_ref[k], f32)
    discount = 1.0 - hg
    rate = discount * (1.0 - tg)
    return jnp.log(rate), jnp.sqrt(1.0 - rate * rate), discount * tg / rate


def powers(log_rate, steps):
    a = jnp.exp(iota((steps // 8, F), 0).astype(f32) * (8.0 * log_rate))
    b = jnp.exp(iota((8, F), 0).astype(f32) * log_rate)
    return (a[:, None, :] * b[None, :, :]).reshape(steps, F)


def ends_before(ended_row, steps):
    ended = jnp.broadcast_to(ended_row, (F, steps)).astype(bf16)
    below = (iota((steps, steps), 1) < iota((steps, steps), 0)).astype(f32).astype(bf16)
    return lax.dot_general(below, ended, (((1,), (1,)), ((), ())), preferred_element_type=f32)


def place_in_cube(i, core):
    gray, half = (i ^ (i >> 1)) & 1, i >> 1
    return (gray, half) if core == 0 else (half, gray)


def local_kernel(hg_hbm, tg_hbm, end_hbm, s_hbm, wf_hbm, w_hbm, r_ref, st_ref, g_ref, msg_ref, rate_ref, open_ref,
                 hg_ref, tg_ref, end_ref, s_ref, wf_ref, w_ref, sems):
    blocks, _, blk = w_ref.shape
    steps, width = s_ref.shape
    num_k = hg_ref.shape[0]
    kf = blocks * blk
    copies = [
        pltpu.make_async_copy(a, b, sems.at[n])
        for n, (a, b) in enumerate(
            [(hg_hbm, hg_ref), (tg_hbm, tg_ref), (end_hbm, end_ref), (s_hbm, s_ref), (wf_hbm, wf_ref)]
            + [(w_hbm.at[:, i * blk : (i + 1) * blk], w_ref.at[i]) for i in range(blocks)]
        )
    ]
    for copy in copies:
        copy.start()
    for copy in copies[:3]:
        copy.wait()
    ended_row = end_ref[...].astype(f32)
    rows, cols = iota((steps, steps), 0), iota((steps, steps), 1)
    at_row = ends_before(ended_row, steps)
    ended = jnp.broadcast_to(ended_row, (steps, steps)).astype(bf16)
    above = (rows < cols).astype(f32).astype(bf16)
    at_col = jnp.dot(ended, above, preferred_element_type=f32)
    at_rows = jnp.concatenate([at_row] * (steps // F), axis=1)
    mask = jnp.where((at_rows == at_col) & (cols >= rows), 1.0, 0.0).astype(bf16)
    total = jnp.sum(ended_row, axis=1, keepdims=True)
    still = jnp.where(at_row == total, 1.0, 0.0)
    open_ref[...] = still
    for z in range(msg_ref.shape[0]):
        msg_ref[z, num_k:, :] = jnp.broadcast_to(jnp.where(total == 0.0, 1.0, 0.0), (msg_ref.shape[1] - num_k, F))
    lane = iota((1, F), 1)
    by_lane = jnp.zeros((1, F), f32)
    for k in range(num_k):
        log_rate = coefficients(hg_ref, tg_ref, k)[0]
        rate_ref[k : k + 1, :] = log_rate
        by_lane = jnp.where(lane % num_k == k, log_rate, by_lane)
    rate_ref[num_k:, :] = jnp.broadcast_to(by_lane, (8, F))
    r_ref[:, kf : kf + F] = (still * backwards(by_lane, steps)).astype(bf16)

    for copy in copies[3:5]:
        copy.wait()
    s = s_ref[...]
    f = jnp.dot(s, wf_ref[...], preferred_element_type=f32)
    per = blk // F

    def predict(i):
        copies[5 + i].wait()
        return jnp.dot(s, w_ref[i], preferred_element_type=f32).astype(bf16)

    def turn():
        st = s.T
        here = lax.axis_index("c")
        label = {(a, core): place_in_cube(lax.axis_index(a), core)[0] for a in ("y", "x") for core in range(2)}
        tall = st_ref.shape[0] // (SIZES[1] * SIZES[2])
        for n in range(st.shape[0] // tall):
            y, x, core = n // (SIZES[2] * SIZES[3]), n // SIZES[3] % SIZES[2], n % SIZES[3]
            (ly, iy), (lx, ix) = place_in_cube(y, core), place_in_cube(x, core)
            at = ((ly ^ label["y", core]) * 2 + (lx ^ label["x", core])) * 4 + iy * 2 + ix
            part = st[n * tall : (n + 1) * tall, :]

            @pl.when(here == core)
            def _():
                st_ref[pl.ds(pl.multiple_of(at * tall, tall), tall), :] = part

            @pl.when(here != core)
            def _():
                left = kf + F + at // (steps // tall) * steps
                r_ref[pl.ds(pl.multiple_of(at % (steps // tall) * tall, tall), tall), pl.ds(pl.multiple_of(left, F), steps)] = part

    turn()
    following = predict(0)
    for i in range(blocks):
        pred = following
        if i + 1 < blocks:
            following = predict(i + 1)
        scaled, backs, biased = [], [], []
        for j in range(per):
            log_rate, scale, beta = coefficients(hg_ref, tg_ref, i * per + j)
            p = pred[:, j * F : (j + 1) * F].astype(f32)
            biased.append((p, beta * p))
            scaled.append(powers(log_rate, steps) * (scale * f + biased[j][1]))
            backs.append(powers(-log_rate, steps))
        scaled = jnp.concatenate(scaled, axis=1)
        high = scaled.astype(bf16)
        low = (scaled - high.astype(f32)).astype(bf16)
        sums = jnp.dot(mask, high, preferred_element_type=f32)
        sums = sums + jnp.dot(mask, low, preferred_element_type=f32)
        for j in range(per):
            k = i * per + j
            cols = slice(k * F, (k + 1) * F)
            h = backs[j] * sums[:, j * F : (j + 1) * F]
            g = h - biased[j][1]
            g_ref[:, cols] = g
            r_ref[:, cols] = (biased[j][0] - g).astype(bf16)
            for z in range(msg_ref.shape[0]):
                msg_ref[z, k : k + 1, :] = h[:1]


def carry_in(msg_ref, rate_ref, steps):
    here = lax.axis_index("z")
    num_k = rate_ref.shape[0] - 8
    through = jnp.exp(steps * rate_ref[:num_k, :])
    later = jnp.zeros((num_k, F), f32)
    for z in range(msg_ref.shape[0] - 1, 0, -1):
        block = msg_ref[z, :num_k, :] + through * msg_ref[z, num_k : num_k + 1, :] * later
        later = jnp.where(z > here, block, later)
    return later


def backwards(log_rate, steps):
    return jnp.exp(steps * log_rate) * powers(-log_rate, steps)


def returns_kernel(msg_ref, rate_ref, open_ref, g_ref, out_ref, h_ref):
    steps = g_ref.shape[0]
    per = g_ref.shape[1] // F
    i = pl.program_id(0)

    @pl.when(i == 0)
    def _():
        h_ref[...] = carry_in(msg_ref, rate_ref, steps)

    still = open_ref[...]
    for j in range(per):
        k = pl.ds(i * per + j, 1)
        cols = slice(j * F, (j + 1) * F)
        decay = still * backwards(rate_ref[k, :], steps)
        out_ref[:, cols] = (g_ref[:, cols] + decay * h_ref[k, :]).astype(bf16)


def grad_kernel(dz, st_ref, r_ref, ro_ref, msg_ref, msgo_ref, rate_ref, *outs):
    tall, steps = st_ref.shape
    halves, quads, rows, cols = outs[0].shape
    num_k = rate_ref.shape[0] - 8
    kf = num_k * F
    st = st_ref[...]
    sto = jnp.concatenate([ro_ref[:, at : at + steps] for at in range(kf + F, ro_ref.shape[1], steps)], axis=0)
    lane = iota((tall, F), 1)
    a = jnp.dot(st, r_ref[:, kf : kf + F], preferred_element_type=f32)
    a = jnp.where(lane < num_k, a, jnp.dot(sto, ro_ref[:, kf : kf + F], preferred_element_type=f32)).astype(bf16)
    h = [carry_in(ref, rate_ref, steps) for ref in (msg_ref, msgo_ref)]
    h = jnp.concatenate(h + [jnp.zeros((F - 2 * num_k, F), f32)], axis=0)
    row = iota((F, F), 0)
    pz = (lax.axis_index("z") + dz) % 2
    for half in range(halves):
        z = 2 * half + pz
        at = pl.ds(pl.multiple_of(z * cols, cols), cols)
        of_k = [z * (cols // F) + j for j in range(cols // F)]
        h_k = [jnp.where((row == k) | (row == k + num_k), h, 0.0) for k in of_k]
        g = jnp.dot(st, r_ref[:, at], preferred_element_type=f32)
        g = g + jnp.dot(sto, ro_ref[:, at], preferred_element_type=f32)
        g = g - jnp.dot(a, jnp.concatenate(h_k, axis=1).astype(bf16), preferred_element_type=f32)
        g = g.astype(bf16).reshape(len(outs), quads, rows, cols)
        for n, out in enumerate(outs):
            out[half] = g[n]


def cube_kernel(*refs):
    *ins, out_ref = refs
    for half in range(out_ref.shape[0]):
        total = ins[0][half].astype(f32)
        for ref in ins[1:]:
            total = total + ref[half].astype(f32)
        out_ref[half] = total.astype(out_ref.dtype)


def final_kernel(norm, x_ref, y_ref):
    y_ref[...] = jnp.sum(x_ref[...].astype(f32), axis=0) * norm


def whole(shape):
    return pl.BlockSpec(shape, lambda i: (0,) * len(shape))


def params(mib):
    return pltpu.CompilerParams(vmem_limit_bytes=mib * MIB)


def flat(place):
    n = 0
    for i, size in zip(place, SIZES):
        n = n * size + i
    return n


def across(offset):
    pairs = []
    for place in itertools.product(*(range(n) for n in SIZES)):
        core = place[3]
        to = [
            i if not d else (i ^ 1 if core == 0 else ((i + 1) % n if i % 2 else (i - 1) % n))
            for i, d, n in zip(place, offset, SIZES)
        ]
        pairs.append((flat(place), flat(to + [core])))
    return pairs


def alike():
    def place(core, label, index):
        if core == 0:
            return 3 - label if index else label
        return 3 - index if label else index

    return [
        [flat((2 * z + pz, place(c, py, y), place(c, px, x), c)) for z in range(4) for y in range(2) for x in range(2)]
        for c in range(2)
        for pz, py, px in OFFSETS
    ]


def body(states, episode_end, feature_head, successor_head, horizon_gap, trace_gap):
    steps, width = states.shape[1:]
    num_k = horizon_gap.shape[0]
    kf = successor_head.shape[1]
    nz, ny, nx, nc = SIZES
    swap = [(0, 1), (1, 0)]
    blk = 4 * F
    n = kf // blk
    rows, cols = width // (ny * nx * nc), kf // nz
    half, parts, quads = nz // 2, 4, ny * nx // 4
    tall = parts * quads * rows
    shape = jax.ShapeDtypeStruct
    resid, st, g_local, msg, rates, still_open = pl.pallas_call(
        local_kernel,
        in_specs=[HBM] * 6,
        out_specs=[VMEM] * 6,
        out_shape=[
            shape((steps, kf + F + tall), bf16),
            shape((tall, steps), bf16),
            shape((steps, kf), f32),
            shape((nz, num_k + 8, F), f32),
            shape((num_k + 8, F), f32),
            shape((steps, F), f32),
        ],
        scratch_shapes=[
            pltpu.SMEM((num_k,), f32),
            pltpu.SMEM((num_k,), f32),
            pltpu.VMEM((1, steps), jnp.int32),
            pltpu.VMEM((steps, width), bf16),
            pltpu.VMEM((width, F), bf16),
            pltpu.VMEM((n, width, blk), bf16),
            pltpu.SemaphoreType.DMA((5 + n,)),
        ],
        compiler_params=params(48),
        name="local",
    )(*[
        pltpu.with_memory_space_constraint(array, pltpu.HBM)
        for array in (horizon_gap, trace_gap, episode_end, states[0], feature_head, successor_head)
    ])
    resid_other = lax.ppermute(resid, "c", swap)
    msg = lax.all_to_all(msg, "z", 0, 0, tiled=True)
    msg_other = lax.ppermute(msg, "c", swap)
    chunk = (half, quads, rows, cols)

    def grads(dz):
        return pl.pallas_call(
            functools.partial(grad_kernel, dz),
            in_specs=[VMEM] * 6,
            out_specs=[VMEM] * 4,
            out_shape=[shape(chunk, bf16)] * 4,
            compiler_params=params(12),
            name="grad",
        )(st, resid, resid_other, msg, msg_other, rates)

    far, near = grads(1), grads(0)
    chunks = near + far
    chunks = dict(zip(OFFSETS, chunks))
    sums = [chunks[0, 0, 0]] + [lax.ppermute(chunks[o], AXES, across(o)) for o in ORDER]
    returns = pl.pallas_call(
        returns_kernel,
        grid=(n,),
        in_specs=[VMEM] * 3 + [pl.BlockSpec((steps, blk), lambda i: (0, i))],
        out_specs=pl.BlockSpec((steps, blk), lambda i: (0, i)),
        out_shape=shape((steps, kf), bf16),
        scratch_shapes=[pltpu.VMEM((num_k, F), f32)],
        compiler_params=params(12),
        name="returns",
    )(msg, rates, still_open, g_local)
    returns, *sums = lax.optimization_barrier((returns, *sums))
    grad = pl.pallas_call(
        cube_kernel,
        in_specs=[VMEM] * 8,
        out_specs=VMEM,
        out_shape=shape(chunk, bf16),
        compiler_params=params(12),
        name="sum_cube",
    )(*sums)
    grad = lax.all_to_all(grad.reshape(-1, rows, cols), AXES, 0, 0, axis_index_groups=alike())
    norm = float(steps * nz * ny * nx * nc) ** -0.5
    head_grad = pl.pallas_call(
        functools.partial(final_kernel, norm),
        in_specs=[VMEM],
        out_specs=VMEM,
        out_shape=shape((rows, cols), f32),
        compiler_params=params(4),
        name="sum_rest",
    )(grad)
    return returns[None], head_grad


def solution(mesh):
    grid = Mesh(mesh.devices.reshape(SIZES), AXES)
    traj = ("y", "x", "c")
    return jax.shard_map(
        body,
        mesh=grid,
        in_specs=(P(traj, "z", None), P(traj, "z"), P(), P(), P(), P()),
        out_specs=(P(traj, "z", None), P(traj, "z")),
        check_vma=False,
    )
```

```python
import functools
import itertools
import jax
import jax.numpy as jnp
from jax import lax
from jax.experimental import pallas as pl
from jax.experimental.pallas import tpu as pltpu
from jax.sharding import Mesh, PartitionSpec as P

F = 128
EARLY = 5
MIB = 1 << 20
AXES = ("z", "y", "x", "c")
SIZES = (8, 4, 4, 2)
f32, bf16 = jnp.float32, jnp.bfloat16
SMEM = pl.BlockSpec(memory_space=pltpu.SMEM)
VMEM = pl.BlockSpec(memory_space=pltpu.VMEM)
HBM = pl.BlockSpec(memory_space=pltpu.HBM)
OFFSETS = list(itertools.product((0, 1), repeat=3))


def iota(shape, dim):
    return lax.broadcasted_iota(jnp.int32, shape, dim)


def coefficients(hg_ref, tg_ref, k):
    hg = jnp.full((1, F), hg_ref[k], f32)
    tg = jnp.full((1, F), tg_ref[k], f32)
    discount = 1.0 - hg
    rate = discount * (1.0 - tg)
    return jnp.log(rate), jnp.sqrt(1.0 - rate * rate), discount * tg / rate


def powers(log_rate, steps):
    a = jnp.exp(iota((steps // 8, F), 0).astype(f32) * (8.0 * log_rate))
    b = jnp.exp(iota((8, F), 0).astype(f32) * log_rate)
    return (a[:, None, :] * b[None, :, :]).reshape(steps, F)


def ends_before(ended_row, steps):
    ended = jnp.broadcast_to(ended_row, (F, steps)).astype(bf16)
    below = (iota((steps, steps), 1) < iota((steps, steps), 0)).astype(f32).astype(bf16)
    return lax.dot_general(below, ended, (((1,), (1,)), ((), ())), preferred_element_type=f32)


def place_in_cube(i, core):
    gray, half = (i ^ (i >> 1)) & 1, i >> 1
    return (gray, half) if core == 0 else (half, gray)


def local_kernel(hg_hbm, tg_hbm, end_hbm, s_hbm, wf_hbm, w_hbm, r_ref, st_ref, g_ref, msg_ref, rate_ref, open_ref,
                 hg_ref, tg_ref, end_ref, s_ref, wf_ref, w_ref, sems):
    blocks, _, blk = w_ref.shape
    steps, width = s_ref.shape
    num_k = hg_ref.shape[0]
    kf = blocks * blk
    copies = [
        pltpu.make_async_copy(a, b, sems.at[n])
        for n, (a, b) in enumerate(
            [(hg_hbm, hg_ref), (tg_hbm, tg_ref), (end_hbm, end_ref), (s_hbm, s_ref), (wf_hbm, wf_ref)]
            + [(w_hbm.at[:, i * blk : (i + 1) * blk], w_ref.at[i]) for i in range(blocks)]
        )
    ]
    for copy in copies:
        copy.start()
    for copy in copies[:3]:
        copy.wait()
    ended_row = end_ref[...].astype(f32)
    rows, cols = iota((steps, steps), 0), iota((steps, steps), 1)
    at_row = ends_before(ended_row, steps)
    ended = jnp.broadcast_to(ended_row, (steps, steps)).astype(bf16)
    above = (rows < cols).astype(f32).astype(bf16)
    at_col = jnp.dot(ended, above, preferred_element_type=f32)
    at_rows = jnp.concatenate([at_row] * (steps // F), axis=1)
    mask = jnp.where((at_rows == at_col) & (cols >= rows), 1.0, 0.0).astype(bf16)
    total = jnp.sum(ended_row, axis=1, keepdims=True)
    still = jnp.where(at_row == total, 1.0, 0.0)
    open_ref[...] = still
    for z in range(msg_ref.shape[0]):
        msg_ref[z, num_k:, :] = jnp.broadcast_to(jnp.where(total == 0.0, 1.0, 0.0), (msg_ref.shape[1] - num_k, F))
    lane = iota((1, F), 1)
    by_lane = jnp.zeros((1, F), f32)
    for k in range(num_k):
        log_rate = coefficients(hg_ref, tg_ref, k)[0]
        rate_ref[k : k + 1, :] = log_rate
        by_lane = jnp.where(lane % num_k == k, log_rate, by_lane)
    rate_ref[num_k:, :] = jnp.broadcast_to(by_lane, (8, F))
    r_ref[:, kf : kf + F] = (still * backwards(by_lane, steps)).astype(bf16)

    for copy in copies[3:5]:
        copy.wait()
    s = s_ref[...]
    f = jnp.dot(s, wf_ref[...], preferred_element_type=f32)
    per = blk // F

    def predict(i):
        copies[5 + i].wait()
        return jnp.dot(s, w_ref[i], preferred_element_type=f32).astype(bf16)

    def turn():
        st = s.T
        here = lax.axis_index("c")
        tall = st_ref.shape[0] // (SIZES[1] * SIZES[2])
        for n in range(st.shape[0] // tall):
            y, x, core = n // (SIZES[2] * SIZES[3]), n // SIZES[3] % SIZES[2], n % SIZES[3]
            (ly, iy), (lx, ix) = place_in_cube(y, core), place_in_cube(x, core)
            at = (ly * 2 + lx) * 4 + iy * 2 + ix
            part = st[n * tall : (n + 1) * tall, :]

            @pl.when(here == core)
            def _():
                st_ref[at * tall : (at + 1) * tall, :] = part

            @pl.when(here != core)
            def _():
                left, top = kf + F + at // (steps // tall) * steps, at % (steps // tall) * tall
                r_ref[top : top + tall, left : left + steps] = part

    turn()
    following = predict(0)
    for i in range(blocks):
        pred = following
        if i + 1 < blocks:
            following = predict(i + 1)
        scaled, backs, biased = [], [], []
        for j in range(per):
            log_rate, scale, beta = coefficients(hg_ref, tg_ref, i * per + j)
            p = pred[:, j * F : (j + 1) * F].astype(f32)
            biased.append((p, beta * p))
            scaled.append(powers(log_rate, steps) * (scale * f + biased[j][1]))
            backs.append(powers(-log_rate, steps))
        scaled = jnp.concatenate(scaled, axis=1)
        high = scaled.astype(bf16)
        low = (scaled - high.astype(f32)).astype(bf16)
        sums = jnp.dot(mask, high, preferred_element_type=f32)
        sums = sums + jnp.dot(mask, low, preferred_element_type=f32)
        for j in range(per):
            k = i * per + j
            cols = slice(k * F, (k + 1) * F)
            h = backs[j] * sums[:, j * F : (j + 1) * F]
            g = h - biased[j][1]
            g_ref[:, cols] = g
            r_ref[:, cols] = (biased[j][0] - g).astype(bf16)
            for z in range(msg_ref.shape[0]):
                msg_ref[z, k : k + 1, :] = h[:1]


def carry_in(msg_ref, rate_ref, steps):
    here = lax.axis_index("z")
    num_k = rate_ref.shape[0] - 8
    through = jnp.exp(steps * rate_ref[:num_k, :])
    later = jnp.zeros((num_k, F), f32)
    for z in range(msg_ref.shape[0] - 1, 0, -1):
        block = msg_ref[z, :num_k, :] + through * msg_ref[z, num_k : num_k + 1, :] * later
        later = jnp.where(z > here, block, later)
    return later


def backwards(log_rate, steps):
    return jnp.exp(steps * log_rate) * powers(-log_rate, steps)


def returns_kernel(msg_ref, rate_ref, open_ref, g_ref, out_ref, h_ref):
    steps = g_ref.shape[0]
    per = g_ref.shape[1] // F
    i = pl.program_id(0)

    @pl.when(i == 0)
    def _():
        h_ref[...] = carry_in(msg_ref, rate_ref, steps)

    still = open_ref[...]
    for j in range(per):
        k = pl.ds(i * per + j, 1)
        cols = slice(j * F, (j + 1) * F)
        decay = still * backwards(rate_ref[k, :], steps)
        out_ref[:, cols] = (g_ref[:, cols] + decay * h_ref[k, :]).astype(bf16)


def product(st, r_ref, ro_ref, at):
    kf, steps = ro_ref.shape[1] - st.shape[0] - F, st.shape[1]
    sto = jnp.concatenate([ro_ref[:, n : n + steps] for n in range(kf + F, ro_ref.shape[1], steps)], axis=0)
    g = jnp.dot(st, r_ref[:, at], preferred_element_type=f32)
    return g + jnp.dot(sto, ro_ref[:, at], preferred_element_type=f32)


def early_kernel(num_k, st_ref, r_ref, ro_ref, g_ref, a_ref):
    st = st_ref[...]
    kf = num_k * F
    steps = st.shape[1]
    sto = jnp.concatenate([ro_ref[:, n : n + steps] for n in range(kf + F, ro_ref.shape[1], steps)], axis=0)
    lane = iota((st.shape[0], F), 1)
    a = jnp.dot(st, r_ref[:, kf : kf + F], preferred_element_type=f32)
    a_ref[...] = jnp.where(lane < num_k, a, jnp.dot(sto, ro_ref[:, kf : kf + F], preferred_element_type=f32)).astype(bf16)
    cols = g_ref.shape[-1]
    for z in range(g_ref.shape[0]):
        g_ref[z] = product(st, r_ref, ro_ref, slice(z * cols, (z + 1) * cols))


def grad_kernel(st_ref, r_ref, ro_ref, msg_ref, msgo_ref, rate_ref, g_ref, a_ref, out_ref):
    parts, halves, quads, rows, cols = out_ref.shape
    parts //= 2
    num_k = rate_ref.shape[0] - 8
    steps = st_ref.shape[1]
    st = st_ref[...]
    h = [carry_in(ref, rate_ref, steps) for ref in (msg_ref, msgo_ref)]
    h = jnp.concatenate(h + [jnp.zeros((F - 2 * num_k, F), f32)], axis=0)
    row = iota((F, F), 0)
    for z in range(2 * halves):
        of_k = [z * (cols // F) + j for j in range(cols // F)]
        h_k = [jnp.where((row == k) | (row == k + num_k), h, 0.0) for k in of_k]
        g = g_ref[z] if z < g_ref.shape[0] else product(st, r_ref, ro_ref, slice(z * cols, (z + 1) * cols))
        g = g - jnp.dot(a_ref[...], jnp.concatenate(h_k, axis=1).astype(bf16), preferred_element_type=f32)
        g = g.astype(bf16).reshape(parts, quads, rows, cols)
        for n in range(parts):
            out_ref[z % 2 * parts + n, z // 2] = g[n]


def cube_kernel(in_ref, out_ref):
    for half in range(out_ref.shape[0]):
        out_ref[half] = jnp.sum(in_ref[:, half].astype(f32), axis=0).astype(out_ref.dtype)


def final_kernel(norm, x_ref, y_ref):
    y_ref[...] = jnp.sum(x_ref[...].astype(f32), axis=0) * norm


def whole(shape):
    return pl.BlockSpec(shape, lambda i: (0,) * len(shape))


def params(mib):
    return pltpu.CompilerParams(vmem_limit_bytes=mib * MIB)


def flat(place):
    n = 0
    for i, size in zip(place, SIZES):
        n = n * size + i
    return n


def place(core, label, index):
    if core == 0:
        return 3 - label if index else label
    return 3 - index if label else index


def alike():
    return [
        [flat((2 * z + pz, place(c, py, y), place(c, px, x), c)) for z in range(4) for y in range(2) for x in range(2)]
        for c in range(2)
        for pz, py, px in OFFSETS
    ]


def cubes():
    def along(core, label, cube):
        return 2 * cube + label if core == 0 else (2 * cube + 2 - label) % SIZES[0]

    return [
        [flat((along(c, pz, z), place(c, py, y), place(c, px, x), c)) for pz, py, px in OFFSETS]
        for c in range(2)
        for z in range(SIZES[0] // 2)
        for y in range(2)
        for x in range(2)
    ]


def body(states, episode_end, feature_head, successor_head, horizon_gap, trace_gap):
    steps, width = states.shape[1:]
    num_k = horizon_gap.shape[0]
    kf = successor_head.shape[1]
    nz, ny, nx, nc = SIZES
    swap = [(0, 1), (1, 0)]
    blk = 4 * F
    n = kf // blk
    rows, cols = width // (ny * nx * nc), kf // nz
    half, parts, quads = nz // 2, 4, ny * nx // 4
    tall = parts * quads * rows
    shape = jax.ShapeDtypeStruct
    resid, st, g_local, msg, rates, still_open = pl.pallas_call(
        local_kernel,
        in_specs=[HBM] * 6,
        out_specs=[VMEM] * 6,
        out_shape=[
            shape((steps, kf + F + tall), bf16),
            shape((tall, steps), bf16),
            shape((steps, kf), f32),
            shape((nz, num_k + 8, F), f32),
            shape((num_k + 8, F), f32),
            shape((steps, F), f32),
        ],
        scratch_shapes=[
            pltpu.SMEM((num_k,), f32),
            pltpu.SMEM((num_k,), f32),
            pltpu.VMEM((1, steps), jnp.int32),
            pltpu.VMEM((steps, width), bf16),
            pltpu.VMEM((width, F), bf16),
            pltpu.VMEM((n, width, blk), bf16),
            pltpu.SemaphoreType.DMA((5 + n,)),
        ],
        compiler_params=params(48),
        name="local",
    )(*[
        pltpu.with_memory_space_constraint(array, pltpu.HBM)
        for array in (horizon_gap, trace_gap, episode_end, states[0], feature_head, successor_head)
    ])
    resid_other = lax.ppermute(resid, "c", swap)
    msg = lax.all_to_all(msg, "z", 0, 0, tiled=True)
    msg, resid_other = lax.optimization_barrier((msg, resid_other))
    msg_other = lax.ppermute(msg, "c", swap)
    chunk = (half, quads, rows, cols)

    early, factor = pl.pallas_call(
        functools.partial(early_kernel, num_k),
        in_specs=[VMEM] * 3,
        out_specs=[VMEM] * 2,
        out_shape=[shape((EARLY, tall, cols), f32), shape((tall, F), bf16)],
        compiler_params=params(12),
        cost_estimate=pl.CostEstimate(flops=2 * EARLY * tall * steps * cols * 2, bytes_accessed=4 * MIB, transcendentals=0),
        name="early",
    )(st, resid, resid_other)
    grad = pl.pallas_call(
        grad_kernel,
        in_specs=[VMEM] * 8,
        out_specs=VMEM,
        out_shape=shape((2 * parts, *chunk), bf16),
        compiler_params=params(12),
        name="grad",
    )(st, resid, resid_other, msg, msg_other, rates, early, factor)
    grad = lax.all_to_all(grad.reshape(2 * parts, -1, cols), AXES, 0, 0, axis_index_groups=cubes())
    grad = pl.pallas_call(
        cube_kernel,
        in_specs=[VMEM],
        out_specs=VMEM,
        out_shape=shape(chunk, bf16),
        compiler_params=params(12),
        name="sum_cube",
    )(grad.reshape(2 * parts, *chunk))
    grad, msg = lax.optimization_barrier((grad, msg))
    returns = pl.pallas_call(
        returns_kernel,
        grid=(n,),
        in_specs=[VMEM] * 3 + [pl.BlockSpec((steps, blk), lambda i: (0, i))],
        out_specs=pl.BlockSpec((steps, blk), lambda i: (0, i)),
        out_shape=shape((steps, kf), bf16),
        scratch_shapes=[pltpu.VMEM((num_k, F), f32)],
        compiler_params=params(12),
        name="returns",
    )(msg, rates, still_open, g_local)
    grad = lax.all_to_all(grad.reshape(-1, rows, cols), AXES, 0, 0, axis_index_groups=alike())
    norm = float(steps * nz * ny * nx * nc) ** -0.5
    head_grad = pl.pallas_call(
        functools.partial(final_kernel, norm),
        in_specs=[VMEM],
        out_specs=VMEM,
        out_shape=shape((rows, cols), f32),
        compiler_params=params(4),
        name="sum_rest",
    )(grad)
    return returns[None], head_grad


def solution(mesh):
    grid = Mesh(mesh.devices.reshape(SIZES), AXES)
    traj = ("y", "x", "c")
    return jax.shard_map(
        body,
        mesh=grid,
        in_specs=(P(traj, "z", None), P(traj, "z"), P(), P(), P(), P()),
        out_specs=(P(traj, "z", None), P(traj, "z")),
        check_vma=False,
    )
```

```python
import functools
import itertools
import jax
import jax.numpy as jnp
from jax import lax
from jax.experimental import pallas as pl
from jax.experimental.pallas import tpu as pltpu
from jax.sharding import Mesh, PartitionSpec as P

F = 128
MIB = 1 << 20
AXES = ("z", "y", "x", "c")
SIZES = (8, 4, 4, 2)
f32, bf16 = jnp.float32, jnp.bfloat16
SMEM = pl.BlockSpec(memory_space=pltpu.SMEM)
VMEM = pl.BlockSpec(memory_space=pltpu.VMEM)
HBM = pl.BlockSpec(memory_space=pltpu.HBM)
OFFSETS = list(itertools.product((0, 1), repeat=3))


def iota(shape, dim):
    return lax.broadcasted_iota(jnp.int32, shape, dim)


def coefficients(hg_ref, tg_ref, k):
    hg = jnp.full((1, F), hg_ref[k], f32)
    tg = jnp.full((1, F), tg_ref[k], f32)
    discount = 1.0 - hg
    rate = discount * (1.0 - tg)
    return jnp.log(rate), jnp.sqrt(1.0 - rate * rate), discount * tg / rate


def powers(log_rate, steps):
    a = jnp.exp(iota((steps // 8, F), 0).astype(f32) * (8.0 * log_rate))
    b = jnp.exp(iota((8, F), 0).astype(f32) * log_rate)
    return (a[:, None, :] * b[None, :, :]).reshape(steps, F)


def ends_before(ended_row, steps):
    ended = jnp.broadcast_to(ended_row, (F, steps)).astype(bf16)
    below = (iota((steps, steps), 1) < iota((steps, steps), 0)).astype(f32).astype(bf16)
    return lax.dot_general(below, ended, (((1,), (1,)), ((), ())), preferred_element_type=f32)


def place_in_cube(i, core):
    gray, half = (i ^ (i >> 1)) & 1, i >> 1
    return (gray, half) if core == 0 else (half, gray)


def local_kernel(hg_hbm, tg_hbm, end_hbm, s_hbm, wf_hbm, w_hbm, r_ref, st_ref, g_ref, rate_ref, open_ref,
                 hg_ref, tg_ref, end_ref, s_ref, wf_ref, w_ref, sems):
    blocks, _, blk = w_ref.shape
    steps, width = s_ref.shape
    num_k = hg_ref.shape[0]
    kf = blocks * blk
    copies = [
        pltpu.make_async_copy(a, b, sems.at[n])
        for n, (a, b) in enumerate(
            [(hg_hbm, hg_ref), (tg_hbm, tg_ref), (end_hbm, end_ref), (s_hbm, s_ref), (wf_hbm, wf_ref)]
            + [(w_hbm.at[:, i * blk : (i + 1) * blk], w_ref.at[i]) for i in range(blocks)]
        )
    ]
    for copy in copies:
        copy.start()
    for copy in copies[:3]:
        copy.wait()
    ended_row = end_ref[...].astype(f32)
    rows, cols = iota((steps, steps), 0), iota((steps, steps), 1)
    at_row = ends_before(ended_row, steps)
    ended = jnp.broadcast_to(ended_row, (steps, steps)).astype(bf16)
    above = (rows < cols).astype(f32).astype(bf16)
    at_col = jnp.dot(ended, above, preferred_element_type=f32)
    at_rows = jnp.concatenate([at_row] * (steps // F), axis=1)
    mask = jnp.where((at_rows == at_col) & (cols >= rows), 1.0, 0.0).astype(bf16)
    total = jnp.sum(ended_row, axis=1, keepdims=True)
    still = jnp.where(at_row == total, 1.0, 0.0)
    open_ref[...] = still
    free = jnp.where(total == 0.0, 1.0, 0.0)
    lane = iota((1, F), 1)
    by_lane = jnp.zeros((1, F), f32)
    for k in range(num_k):
        log_rate = coefficients(hg_ref, tg_ref, k)[0]
        rate_ref[k : k + 1, :] = log_rate
        by_lane = jnp.where(lane % num_k == k, log_rate, by_lane)
    rate_ref[num_k:, :] = jnp.broadcast_to(by_lane, (8, F))
    r_ref[:, kf : kf + F] = (still * backwards(by_lane, steps)).astype(bf16)

    for copy in copies[3:5]:
        copy.wait()
    s = s_ref[...]
    f = jnp.dot(s, wf_ref[...], preferred_element_type=f32)
    per = blk // F

    def predict(i):
        copies[5 + i].wait()
        return jnp.dot(s, w_ref[i], preferred_element_type=f32).astype(bf16)

    def turn():
        st = s.T
        here = lax.axis_index("c")
        tall = st_ref.shape[0] // (SIZES[1] * SIZES[2])
        for n in range(st.shape[0] // tall):
            y, x, core = n // (SIZES[2] * SIZES[3]), n // SIZES[3] % SIZES[2], n % SIZES[3]
            (ly, iy), (lx, ix) = place_in_cube(y, core), place_in_cube(x, core)
            at = (ly * 2 + lx) * 4 + iy * 2 + ix
            part = st[n * tall : (n + 1) * tall, :]

            @pl.when(here == core)
            def _():
                st_ref[at * tall : (at + 1) * tall, :] = part

            @pl.when(here != core)
            def _():
                left, top = kf + F + at // (steps // tall) * steps, at % (steps // tall) * tall
                r_ref[top : top + tall, left : left + steps] = part

    turn()
    following = predict(0)
    carries = []
    for i in range(blocks):
        pred = following
        if i + 1 < blocks:
            following = predict(i + 1)
        scaled, backs, biased = [], [], []
        for j in range(per):
            log_rate, scale, beta = coefficients(hg_ref, tg_ref, i * per + j)
            p = pred[:, j * F : (j + 1) * F].astype(f32)
            biased.append((p, beta * p))
            scaled.append(powers(log_rate, steps) * (scale * f + biased[j][1]))
            backs.append(powers(-log_rate, steps))
        scaled = jnp.concatenate(scaled, axis=1)
        high = scaled.astype(bf16)
        low = (scaled - high.astype(f32)).astype(bf16)
        sums = jnp.dot(mask, high, preferred_element_type=f32)
        sums = sums + jnp.dot(mask, low, preferred_element_type=f32)
        for j in range(per):
            k = i * per + j
            cols = slice(k * F, (k + 1) * F)
            h = backs[j] * sums[:, j * F : (j + 1) * F]
            g = h - biased[j][1]
            g_ref[:, cols] = g
            r_ref[:, cols] = (biased[j][0] - g).astype(bf16)
            carries.append(h[:1])
    last = r_ref.shape[1] - F
    r_ref[:num_k, last:] = jnp.concatenate(carries, axis=0).astype(bf16)
    r_ref[num_k:, last:] = jnp.broadcast_to(free, (steps - num_k, F)).astype(bf16)


def backwards(log_rate, steps):
    return jnp.exp(steps * log_rate) * powers(-log_rate, steps)


def returns_kernel(rows, rate_ref, open_ref, g_ref, partner_ref, x_ref, out_ref, h_ref):
    steps = g_ref.shape[0]
    per = g_ref.shape[1] // F
    i = pl.program_id(0)

    @pl.when(i == 0)
    def _():
        num_k = h_ref.shape[0]
        z, core = lax.axis_index("z"), lax.axis_index("c")
        (_, iy), (_, ix) = own_place("y"), own_place("x")
        through = jnp.exp(steps * rate_ref[:num_k, :])
        places = x_ref.shape[0] // (SIZES[0] // 2)

        def pair(n):
            block = x_ref[n * places + iy * 2 + ix, rows + 16 :, :].astype(f32)
            return block[:, F:], block[:, F - 32 : F - 31]

        later = jnp.where((core == 1) & (z % 2 == 0), pair(0)[0], 0.0)
        for n in range(SIZES[0] // 2 - 1, 0, -1):
            carry, free = pair(n)
            later = jnp.where(n > z // 2, carry + through * through * free * later, later)
        after = partner_ref[:num_k, :] + through * partner_ref[num_k : num_k + 1, :] * later
        h_ref[...] = jnp.where((z % 2 == core) & (z < SIZES[0] - 1), after, later)

    still = open_ref[...]
    for j in range(per):
        k = pl.ds(i * per + j, 1)
        cols = slice(j * F, (j + 1) * F)
        decay = still * backwards(rate_ref[k, :], steps)
        out_ref[:, cols] = (g_ref[:, cols] + decay * h_ref[k, :]).astype(bf16)


def own_place(axis):
    here = lax.axis_index(axis)
    return tuple(
        jnp.where(lax.axis_index("c") == 0, a, b) for a, b in zip(place_in_cube(here, 0), place_in_cube(here, 1))
    )


def grad_kernel(num_k, st_ref, r_ref, ro_ref, out_ref):
    tall, steps = st_ref.shape
    labels, deep, cols = out_ref.shape
    parts, per = labels // 2, cols // F
    part = tall // parts
    kf = num_k * F
    halves = kf // cols // 2
    last = r_ref.shape[1] - F
    st = st_ref[...]
    sto = jnp.concatenate([ro_ref[:, n : n + steps] for n in range(kf + F, last, steps)], axis=0)
    lane = iota((tall, F), 1)
    a = jnp.dot(st, r_ref[:, kf : kf + F], preferred_element_type=f32)
    a = jnp.where(lane < num_k, a, jnp.dot(sto, ro_ref[:, kf : kf + F], preferred_element_type=f32))
    at = a.T
    carries = [ref[: num_k + 1, last:].astype(f32) for ref in (r_ref, ro_ref)]
    for z in range(2 * halves):
        columns = slice(z * cols, (z + 1) * cols)
        g = jnp.dot(st, r_ref[:, columns], preferred_element_type=f32)
        g = g + jnp.dot(sto, ro_ref[:, columns], preferred_element_type=f32)
        g = g.astype(bf16)
        for n in range(parts):
            out_ref[z % 2 * parts + n, z // 2 * part : (z // 2 + 1) * part, :] = g[n * part : (n + 1) * part]

    def wide(rows):
        return jnp.concatenate(rows, axis=1)

    for pz in range(2):
        for n in range(parts):
            rows = [
                wide([carries[u][k : k + 1] for k in range((2 * half + pz) * per, (2 * half + pz + 1) * per)])
                for half in range(halves)
                for u in range(2)
            ]
            rows += [
                wide([
                    at[u * num_k + k : u * num_k + k + 1, n * part : (n + 1) * part]
                    for k in range((2 * half + pz) * per, (2 * half + pz + 1) * per)
                ])
                for half in range(halves)
                for u in range(2)
            ]
            rows += [wide([carries[u][num_k : num_k + 1]] * per) for u in range(2)]
            rows.append(jnp.zeros((24 - len(rows), cols), f32))
            rows.append(wide([carries[0][m * 8 : (m + 1) * 8] for m in range(num_k // 8)]))
            out_ref[pz * parts + n, halves * part :, :] = jnp.concatenate(rows, axis=0).astype(bf16)


def cube_kernel(halves, quads, rows, steps, rate_ref, in_ref, out_ref, partner_ref):
    part = quads * rows
    num_k = rate_ref.shape[0] - 8
    extra = in_ref[:, halves * part :, :].astype(f32)
    sources = range(in_ref.shape[0])

    def all_of(first):
        return jnp.concatenate([extra[n, first : first + 2] for n in sources], axis=0)

    def own(n):
        block = in_ref[n, halves * part :, :].astype(f32)
        return jnp.concatenate([block[24:, m * F : (m + 1) * F] for m in range(num_k // 8)], axis=0), block[16:17, :F]

    z, core = lax.axis_index("z"), lax.axis_index("c")
    label = z % 2 * 4 + own_place("y")[0] * 2 + own_place("x")[0]
    (mine, my_free), (other, other_free) = own(label), own(label ^ 4)
    partner_ref[:num_k, :] = other
    partner_ref[num_k:, :] = jnp.broadcast_to(other_free, (8, F))
    first = z % 2 == core
    through = jnp.exp(steps * rate_ref[:num_k, :])
    early, late = jnp.where(first, mine, other), jnp.where(first, other, mine)
    joined = early + through * jnp.where(first, my_free, other_free) * late
    apart = (core == 1) & ((z == 0) | (z == SIZES[0] - 1))
    joined = jnp.where(apart, early, joined)
    both = jnp.broadcast_to(my_free * other_free, (num_k, F))

    free = all_of(4 * halves)
    for half in range(halves):
        total = jnp.sum(in_ref[:, half * part : (half + 1) * part, :].astype(f32), axis=0).astype(bf16)
        carries, at = all_of(2 * half).astype(bf16), all_of(2 * halves + 2 * half)
        for quad in range(quads):
            here = slice(quad * rows, (quad + 1) * rows)
            beside = [at[:, j * F + quad * rows : j * F + (quad + 1) * rows] for j in range(at.shape[1] // F)]
            beside += [free[:, :rows], both[:, :rows], joined]
            out_ref[half * quads + quad, :rows, :] = total[here]
            out_ref[half * quads + quad, rows : rows + 16, :] = carries
            out_ref[half * quads + quad, rows + 16 :, :] = jnp.concatenate(beside, axis=1).astype(bf16)


def final_kernel(norm, steps, rate_ref, x_ref, y_ref):
    rows, cols = y_ref.shape
    per = cols // F
    z_here, core = lax.axis_index("z"), lax.axis_index("c")
    pz = z_here % 2
    nz, places = SIZES[0], x_ref.shape[0] // (SIZES[0] // 2)

    def cube_of(z):
        if z % 2:
            other = jnp.where(pz == 1, (z - 1) // 2, (z + 1) // 2)
        else:
            other = jnp.where(pz == 1, (z // 2 + nz // 2 - 1) % (nz // 2), z // 2)
        return jnp.where(core == 0, z // 2, other) % (nz // 2)

    def units(z, first):
        n, top = cube_of(z), first + z % 2 * 8
        return jnp.concatenate([x_ref[n * places + p, top : top + 8, :].astype(f32) for p in range(places)], axis=0)

    k = [rate_ref[pl.ds(z_here * per + j, 1), :] for j in range(per)]
    through = jnp.exp(steps * jnp.concatenate(k, axis=1))
    later = jnp.zeros((8 * places, cols), f32)
    h, at = [], []
    for z in range(nz - 1, -1, -1):
        beside = units(z, rows + 16)
        h.append(later)
        at.append(beside[:, :F])
        later = units(z, rows) + through * beside[:, per * rows : per * rows + 1] * later
    h = jnp.concatenate(h, axis=0).astype(bf16)
    at = jnp.concatenate(at, axis=0).astype(bf16)
    part = lax.dot_general(at, h, (((0,), (0,)), ((), ())), preferred_element_type=f32)
    part = jnp.concatenate([part[j * rows : (j + 1) * rows, j * F : (j + 1) * F] for j in range(per)], axis=1)
    total = jnp.sum(x_ref[:, :rows, :].astype(f32), axis=0)
    y_ref[...] = (total - part) * norm


def whole(shape):
    return pl.BlockSpec(shape, lambda i: (0,) * len(shape))


def params(mib):
    return pltpu.CompilerParams(vmem_limit_bytes=mib * MIB)


def flat(place):
    n = 0
    for i, size in zip(place, SIZES):
        n = n * size + i
    return n


def place(core, label, index):
    if core == 0:
        return 3 - label if index else label
    return 3 - index if label else index


def alike():
    return [
        [flat((2 * z + pz, place(c, py, y), place(c, px, x), c)) for z in range(4) for y in range(2) for x in range(2)]
        for c in range(2)
        for pz, py, px in OFFSETS
    ]


def cubes():
    def along(core, label, cube):
        return 2 * cube + label if core == 0 else (2 * cube + 2 - label) % SIZES[0]

    return [
        [flat((along(c, pz, z), place(c, py, y), place(c, px, x), c)) for pz, py, px in OFFSETS]
        for c in range(2)
        for z in range(SIZES[0] // 2)
        for y in range(2)
        for x in range(2)
    ]


def body(states, episode_end, feature_head, successor_head, horizon_gap, trace_gap):
    steps, width = states.shape[1:]
    num_k = horizon_gap.shape[0]
    kf = successor_head.shape[1]
    nz, ny, nx, nc = SIZES
    swap = [(0, 1), (1, 0)]
    blk = 4 * F
    n = kf // blk
    rows, cols = width // (ny * nx * nc), kf // nz
    half, parts, quads = nz // 2, 4, ny * nx // 4
    tall = parts * quads * rows
    shape = jax.ShapeDtypeStruct
    resid, st, g_local, rates, still_open = pl.pallas_call(
        local_kernel,
        in_specs=[HBM] * 6,
        out_specs=[VMEM] * 5,
        out_shape=[
            shape((steps, kf + F + tall + F), bf16),
            shape((tall, steps), bf16),
            shape((steps, kf), f32),
            shape((num_k + 8, F), f32),
            shape((steps, F), f32),
        ],
        scratch_shapes=[
            pltpu.SMEM((num_k,), f32),
            pltpu.SMEM((num_k,), f32),
            pltpu.VMEM((1, steps), jnp.int32),
            pltpu.VMEM((steps, width), bf16),
            pltpu.VMEM((width, F), bf16),
            pltpu.VMEM((n, width, blk), bf16),
            pltpu.SemaphoreType.DMA((5 + n,)),
        ],
        compiler_params=params(48),
        name="local",
    )(*[
        pltpu.with_memory_space_constraint(array, pltpu.HBM)
        for array in (horizon_gap, trace_gap, episode_end, states[0], feature_head, successor_head)
    ])
    resid_other = lax.ppermute(resid, "c", swap)
    deep = half * quads * rows + 32
    grad = pl.pallas_call(
        functools.partial(grad_kernel, num_k),
        in_specs=[VMEM] * 3,
        out_specs=VMEM,
        out_shape=shape((2 * parts, deep, cols), bf16),
        compiler_params=params(12),
        name="grad",
    )(st, resid, resid_other)
    grad = lax.all_to_all(grad, AXES, 0, 0, axis_index_groups=cubes())
    grad, partner = pl.pallas_call(
        functools.partial(cube_kernel, half, quads, rows, steps),
        in_specs=[VMEM] * 2,
        out_specs=[VMEM] * 2,
        out_shape=[shape((half * quads, rows + 32, cols), bf16), shape((num_k + 8, F), f32)],
        compiler_params=params(12),
        name="sum_cube",
    )(rates, grad)
    grad = lax.all_to_all(grad, AXES, 0, 0, axis_index_groups=alike())
    returns = pl.pallas_call(
        functools.partial(returns_kernel, rows),
        grid=(n,),
        in_specs=[VMEM] * 2 + [pl.BlockSpec((steps, blk), lambda i: (0, i))] + [VMEM] * 2,
        out_specs=pl.BlockSpec((steps, blk), lambda i: (0, i)),
        out_shape=shape((steps, kf), bf16),
        scratch_shapes=[pltpu.VMEM((num_k, F), f32)],
        compiler_params=params(12),
        name="returns",
    )(rates, still_open, g_local, partner, grad)
    norm = float(steps * nz * ny * nx * nc) ** -0.5
    head_grad = pl.pallas_call(
        functools.partial(final_kernel, norm, steps),
        in_specs=[VMEM] * 2,
        out_specs=VMEM,
        out_shape=shape((rows, cols), f32),
        compiler_params=params(8),
        name="sum_rest",
    )(rates, grad)
    return returns[None], head_grad


def solution(mesh):
    grid = Mesh(mesh.devices.reshape(SIZES), AXES)
    traj = ("y", "x", "c")
    return jax.shard_map(
        body,
        mesh=grid,
        in_specs=(P(traj, "z", None), P(traj, "z"), P(), P(), P(), P()),
        out_specs=(P(traj, "z", None), P(traj, "z")),
        check_vma=False,
    )
```

```python
import functools
import itertools
import jax
import jax.numpy as jnp
from jax import lax
from jax.experimental import pallas as pl
from jax.experimental.pallas import tpu as pltpu
from jax.sharding import Mesh, PartitionSpec as P

F = 128
MIB = 1 << 20
AXES = ("z", "y", "x", "c")
SIZES = (8, 4, 4, 2)
f32, bf16 = jnp.float32, jnp.bfloat16
SMEM = pl.BlockSpec(memory_space=pltpu.SMEM)
VMEM = pl.BlockSpec(memory_space=pltpu.VMEM)
HBM = pl.BlockSpec(memory_space=pltpu.HBM)
OFFSETS = list(itertools.product((0, 1), repeat=3))


def iota(shape, dim):
    return lax.broadcasted_iota(jnp.int32, shape, dim)


def coefficients(hg_ref, tg_ref, k):
    hg = jnp.full((1, F), hg_ref[k], f32)
    tg = jnp.full((1, F), tg_ref[k], f32)
    discount = 1.0 - hg
    rate = discount * (1.0 - tg)
    return jnp.log(rate), jnp.sqrt(1.0 - rate * rate), discount * tg / rate


def powers(log_rate, steps):
    a = jnp.exp(iota((steps // 8, F), 0).astype(f32) * (8.0 * log_rate))
    b = jnp.exp(iota((8, F), 0).astype(f32) * log_rate)
    return (a[:, None, :] * b[None, :, :]).reshape(steps, F)


def ends_before(ended_row, steps):
    ended = jnp.broadcast_to(ended_row, (F, steps)).astype(bf16)
    below = (iota((steps, steps), 1) < iota((steps, steps), 0)).astype(f32).astype(bf16)
    return lax.dot_general(below, ended, (((1,), (1,)), ((), ())), preferred_element_type=f32)


def place_in_cube(i, core):
    gray, half = (i ^ (i >> 1)) & 1, i >> 1
    return (gray, half) if core == 0 else (half, gray)


def scan_block(first, top, pred, f, mask, rate_ref, coef_ref, r_ref, g_ref):
    steps = pred.shape[0]
    per, num_k = pred.shape[1] // F, coef_ref.shape[0] // 2
    scaled, backs, biased, carries = [], [], [], []
    for j in range(per):
        k = first + j
        log_rate, scale = rate_ref[k : k + 1, :], coef_ref[k : k + 1, :]
        p = pred[:, j * F : (j + 1) * F].astype(f32)
        biased.append((p, coef_ref[num_k + k : num_k + k + 1, :] * p))
        scaled.append(powers(log_rate, steps) * (scale * f + biased[j][1]))
        backs.append(powers(-log_rate, steps))
    scaled = jnp.concatenate(scaled, axis=1)
    high = scaled.astype(bf16)
    low = (scaled - high.astype(f32)).astype(bf16)
    sums = jnp.dot(mask, high, preferred_element_type=f32)
    sums = sums + jnp.dot(mask, low, preferred_element_type=f32)
    for j in range(per):
        cols = slice((first - top + j) * F, (first - top + j + 1) * F)
        h = backs[j] * sums[:, j * F : (j + 1) * F]
        g = h - biased[j][1]
        g_ref[:, cols] = g
        r_ref[:, cols] = (biased[j][0] - g).astype(bf16)
        carries.append(h[:1])
    return carries


def local_kernel(hg_hbm, tg_hbm, end_hbm, s_hbm, wf_hbm, w_hbm, r_ref, st_ref, g_ref, rate_ref, open_ref, coef_ref,
                 f_ref, mask_ref, s_ref, wl_ref, hg_ref, tg_ref, end_ref, wf_ref, w_ref, sems):
    blocks, _, blk = w_ref.shape
    steps, width = s_ref.shape
    num_k = hg_ref.shape[0]
    half = blocks * blk
    copies = [
        pltpu.make_async_copy(a, b, sems.at[n])
        for n, (a, b) in enumerate(
            [(hg_hbm, hg_ref), (tg_hbm, tg_ref), (end_hbm, end_ref), (s_hbm, s_ref), (wf_hbm, wf_ref)]
            + [(w_hbm.at[:, i * blk : (i + 1) * blk], w_ref.at[i]) for i in range(blocks)]
            + [(w_hbm.at[:, half:], wl_ref)]
        )
    ]
    for copy in copies:
        copy.start()
    for copy in copies[:3]:
        copy.wait()
    ended_row = end_ref[...].astype(f32)
    rows, cols = iota((steps, steps), 0), iota((steps, steps), 1)
    at_row = ends_before(ended_row, steps)
    ended = jnp.broadcast_to(ended_row, (steps, steps)).astype(bf16)
    above = (rows < cols).astype(f32).astype(bf16)
    at_col = jnp.dot(ended, above, preferred_element_type=f32)
    at_rows = jnp.concatenate([at_row] * (steps // F), axis=1)
    mask = jnp.where((at_rows == at_col) & (cols >= rows), 1.0, 0.0).astype(bf16)
    mask_ref[...] = mask
    total = jnp.sum(ended_row, axis=1, keepdims=True)
    still = jnp.where(at_row == total, 1.0, 0.0)
    open_ref[...] = still
    lane = iota((1, F), 1)
    by_lane = jnp.zeros((1, F), f32)
    for k in range(num_k):
        log_rate, scale, beta = coefficients(hg_ref, tg_ref, k)
        rate_ref[k : k + 1, :] = log_rate
        coef_ref[k : k + 1, :] = scale
        coef_ref[num_k + k : num_k + k + 1, :] = beta
        by_lane = jnp.where(lane % num_k == k, log_rate, by_lane)
    rate_ref[num_k:, :] = jnp.broadcast_to(by_lane, (8, F))
    r_ref[:, half : half + F] = (still * backwards(by_lane, steps)).astype(bf16)

    for copy in copies[3:5]:
        copy.wait()
    s = s_ref[...]
    f = jnp.dot(s, wf_ref[...], preferred_element_type=f32)
    f_ref[...] = f
    st = s.T
    here = lax.axis_index("c")
    tall = st_ref.shape[0] // (SIZES[1] * SIZES[2])
    for n in range(st.shape[0] // tall):
        y, x, core = n // (SIZES[2] * SIZES[3]), n // SIZES[3] % SIZES[2], n % SIZES[3]
        (ly, iy), (lx, ix) = place_in_cube(y, core), place_in_cube(x, core)
        at = (ly * 2 + lx) * 4 + iy * 2 + ix
        part = st[n * tall : (n + 1) * tall, :]

        @pl.when(here == core)
        def _():
            st_ref[at * tall : (at + 1) * tall, :] = part

        @pl.when(here != core)
        def _():
            left, top = half + F + at // (steps // tall) * steps, at % (steps // tall) * tall
            r_ref[top : top + tall, left : left + steps] = part

    def predict(i):
        copies[5 + i].wait()
        return jnp.dot(s, w_ref[i], preferred_element_type=f32).astype(bf16)

    following = predict(0)
    carries = []
    for i in range(blocks):
        pred = following
        if i + 1 < blocks:
            following = predict(i + 1)
        carries += scan_block(i * blk // F, 0, pred, f, mask, rate_ref, coef_ref, r_ref, g_ref)
    last = r_ref.shape[1] - F
    free = jnp.where(total == 0.0, 1.0, 0.0)
    carries += [jnp.zeros((num_k - len(carries), F), f32)]
    r_ref[:num_k, last:] = jnp.concatenate(carries, axis=0).astype(bf16)
    r_ref[num_k:, last:] = jnp.broadcast_to(free, (steps - num_k, F)).astype(bf16)
    copies[-1].wait()


def rest_kernel(s_ref, w_ref, f_ref, mask_ref, rate_ref, coef_ref, r_ref, g_ref):
    num_k = coef_ref.shape[0] // 2
    half = w_ref.shape[1]
    blk = half // 2
    carries = []
    for i in range(2):
        pred = jnp.dot(s_ref[...], w_ref[:, i * blk : (i + 1) * blk], preferred_element_type=f32).astype(bf16)
        first = num_k - half // F
        carries += scan_block(first + i * blk // F, first, pred, f_ref[...], mask_ref[...], rate_ref, coef_ref, r_ref, g_ref)
    carries += [jnp.zeros((num_k - len(carries), F), f32)]
    r_ref[:num_k, half:] = jnp.concatenate(carries, axis=0).astype(bf16)
    r_ref[num_k:, half:] = jnp.zeros((r_ref.shape[0] - num_k, F), bf16)


def backwards(log_rate, steps):
    return jnp.exp(steps * log_rate) * powers(-log_rate, steps)


def own_place(axis):
    here = lax.axis_index(axis)
    return tuple(
        jnp.where(lax.axis_index("c") == 0, a, b) for a, b in zip(place_in_cube(here, 0), place_in_cube(here, 1))
    )


def columns_of(st, sto, r_ref, ro_ref, at):
    g = jnp.dot(st, r_ref[:, at], preferred_element_type=f32)
    return (g + jnp.dot(sto, ro_ref[:, at], preferred_element_type=f32)).astype(bf16)


def early_kernel(num_k, st_ref, r_ref, ro_ref, g_ref, sto_ref, at_ref):
    tall, steps = st_ref.shape
    count, _, cols = g_ref.shape
    half, last = count * cols, r_ref.shape[1] - F
    st = st_ref[...]
    sto = jnp.concatenate([ro_ref[:, n : n + steps] for n in range(half + F, last, steps)], axis=0)
    sto_ref[...] = sto
    lane = iota((tall, F), 1)
    a = jnp.dot(st, r_ref[:, half : half + F], preferred_element_type=f32)
    a = jnp.where(lane < num_k, a, jnp.dot(sto, ro_ref[:, half : half + F], preferred_element_type=f32))
    at_ref[...] = a.T
    for z in range(count):
        g_ref[z] = columns_of(st, sto, r_ref, ro_ref, slice(z * cols, (z + 1) * cols))


def grad_kernel(num_k, st_ref, sto_ref, r_ref, ro_ref, rl_ref, rlo_ref, g_ref, at_ref, out_ref):
    tall, steps = st_ref.shape
    labels, deep, cols = out_ref.shape
    count = g_ref.shape[0]
    parts, per = labels // 2, cols // F
    part = tall // parts
    halves = num_k * F // cols // 2
    st, sto, at = st_ref[...], sto_ref[...], at_ref[...]
    last = r_ref.shape[1] - F
    carries = []
    for first, second in ((r_ref, rl_ref), (ro_ref, rlo_ref)):
        a, b = first[: num_k + 1, last:].astype(f32), second[: num_k // 2, count * cols :].astype(f32)
        carries.append(jnp.concatenate([a[: num_k // 2], b, a[num_k:]], axis=0))
    for z in range(2 * halves):
        at_z = slice((z - count) * cols, (z - count + 1) * cols)
        g = g_ref[z] if z < count else columns_of(st, sto, rl_ref, rlo_ref, at_z)
        for n in range(parts):
            out_ref[z % 2 * parts + n, z // 2 * part : (z // 2 + 1) * part, :] = g[n * part : (n + 1) * part]

    def wide(rows):
        return jnp.concatenate(rows, axis=1)

    for pz in range(2):
        for n in range(parts):
            rows = [
                wide([carries[u][k : k + 1] for k in range((2 * half + pz) * per, (2 * half + pz + 1) * per)])
                for half in range(halves)
                for u in range(2)
            ]
            rows += [
                wide([
                    at[u * num_k + k : u * num_k + k + 1, n * part : (n + 1) * part]
                    for k in range((2 * half + pz) * per, (2 * half + pz + 1) * per)
                ])
                for half in range(halves)
                for u in range(2)
            ]
            rows += [wide([carries[u][num_k : num_k + 1]] * per) for u in range(2)]
            rows.append(jnp.zeros((24 - len(rows), cols), f32))
            rows.append(wide([carries[0][m * 8 : (m + 1) * 8] for m in range(num_k // 8)]))
            out_ref[pz * parts + n, halves * part :, :] = jnp.concatenate(rows, axis=0).astype(bf16)


def cube_kernel(halves, quads, rows, steps, rate_ref, in_ref, out_ref, partner_ref):
    part = quads * rows
    num_k = rate_ref.shape[0] - 8
    extra = in_ref[:, halves * part :, :].astype(f32)
    sources = range(in_ref.shape[0])

    def all_of(first):
        return jnp.concatenate([extra[n, first : first + 2] for n in sources], axis=0)

    def own(n):
        block = in_ref[n, halves * part :, :].astype(f32)
        return jnp.concatenate([block[24:, m * F : (m + 1) * F] for m in range(num_k // 8)], axis=0), block[16:17, :F]

    z, core = lax.axis_index("z"), lax.axis_index("c")
    label = z % 2 * 4 + own_place("y")[0] * 2 + own_place("x")[0]
    (mine, my_free), (other, other_free) = own(label), own(label ^ 4)
    partner_ref[:num_k, :] = other
    partner_ref[num_k:, :] = jnp.broadcast_to(other_free, (8, F))
    first = z % 2 == core
    through = jnp.exp(steps * rate_ref[:num_k, :])
    early, late = jnp.where(first, mine, other), jnp.where(first, other, mine)
    joined = early + through * jnp.where(first, my_free, other_free) * late
    apart = (core == 1) & ((z == 0) | (z == SIZES[0] - 1))
    joined = jnp.where(apart, early, joined)
    both = jnp.broadcast_to(my_free * other_free, (num_k, F))

    free = all_of(4 * halves)
    for half in range(halves):
        total = jnp.sum(in_ref[:, half * part : (half + 1) * part, :].astype(f32), axis=0).astype(bf16)
        carries, at = all_of(2 * half).astype(bf16), all_of(2 * halves + 2 * half)
        for quad in range(quads):
            here = slice(quad * rows, (quad + 1) * rows)
            beside = [at[:, j * F + quad * rows : j * F + (quad + 1) * rows] for j in range(at.shape[1] // F)]
            beside += [free[:, :rows], both[:, :rows], joined]
            out_ref[half * quads + quad, :rows, :] = total[here]
            out_ref[half * quads + quad, rows : rows + 16, :] = carries
            out_ref[half * quads + quad, rows + 16 :, :] = jnp.concatenate(beside, axis=1).astype(bf16)


def final_kernel(norm, rate_ref, open_ref, g_ref, gl_ref, partner_ref, x_ref, out_hbm, y_hbm, out_ref, y_ref, sems):
    rows, cols = y_ref.shape
    per = cols // F
    steps, kf = out_ref.shape
    num_k = rate_ref.shape[0] - 8
    nz, places = SIZES[0], x_ref.shape[0] // (SIZES[0] // 2)
    z_here, core = lax.axis_index("z"), lax.axis_index("c")
    pz = z_here % 2
    (_, iy), (_, ix) = own_place("y"), own_place("x")

    def pair(n):
        block = x_ref[n * places + iy * 2 + ix, rows + 16 :, :].astype(f32)
        return block[:, F:], block[:, F - 32 : F - 31]

    through = jnp.exp(steps * rate_ref[:num_k, :])
    later = jnp.where((core == 1) & (pz == 0), pair(0)[0], 0.0)
    for n in range(nz // 2 - 1, 0, -1):
        carry, free = pair(n)
        later = jnp.where(n > z_here // 2, carry + through * through * free * later, later)
    after = partner_ref[:num_k, :] + through * partner_ref[num_k : num_k + 1, :] * later
    h = jnp.where((pz == core) & (z_here < nz - 1), after, later)
    still = open_ref[...]
    copies = []
    for k in range(num_k):
        at = slice(k * F, (k + 1) * F)
        decay = still * backwards(rate_ref[k : k + 1, :], steps)
        g = g_ref[:, at] if k < num_k // 2 else gl_ref[:, (k - num_k // 2) * F : (k - num_k // 2 + 1) * F]
        out_ref[:, at] = (g + decay * h[k : k + 1, :]).astype(bf16)
        if k % per == per - 1:
            at = slice((k + 1 - per) * F, (k + 1) * F)
            copies.append(pltpu.make_async_copy(out_ref.at[:, at], out_hbm.at[:, at], sems.at[len(copies)]))
            copies[-1].start()

    def cube_of(z):
        if z % 2:
            other = jnp.where(pz == 1, (z - 1) // 2, (z + 1) // 2)
        else:
            other = jnp.where(pz == 1, (z // 2 + nz // 2 - 1) % (nz // 2), z // 2)
        return jnp.where(core == 0, z // 2, other) % (nz // 2)

    def units(z, first):
        n, top = cube_of(z), first + z % 2 * 8
        return jnp.concatenate([x_ref[n * places + p, top : top + 8, :].astype(f32) for p in range(places)], axis=0)

    k = [rate_ref[pl.ds(z_here * per + j, 1), :] for j in range(per)]
    through = jnp.exp(steps * jnp.concatenate(k, axis=1))
    later = jnp.zeros((8 * places, cols), f32)
    h, at = [], []
    for z in range(nz - 1, -1, -1):
        beside = units(z, rows + 16)
        h.append(later)
        at.append(beside[:, :F])
        later = units(z, rows) + through * beside[:, per * rows : per * rows + 1] * later
    h = jnp.concatenate(h, axis=0).astype(bf16)
    at = jnp.concatenate(at, axis=0).astype(bf16)
    part = lax.dot_general(at, h, (((0,), (0,)), ((), ())), preferred_element_type=f32)
    part = jnp.concatenate([part[j * rows : (j + 1) * rows, j * F : (j + 1) * F] for j in range(per)], axis=1)
    total = jnp.sum(x_ref[:, :rows, :].astype(f32), axis=0)
    y_ref[...] = (total - part) * norm
    copies.append(pltpu.make_async_copy(y_ref, y_hbm, sems.at[len(copies)]))
    copies[-1].start()
    for copy in copies:
        copy.wait()


def whole(shape):
    return pl.BlockSpec(shape, lambda i: (0,) * len(shape))


def params(mib):
    return pltpu.CompilerParams(vmem_limit_bytes=mib * MIB)


def flat(place):
    n = 0
    for i, size in zip(place, SIZES):
        n = n * size + i
    return n


def place(core, label, index):
    if core == 0:
        return 3 - label if index else label
    return 3 - index if label else index


def alike():
    return [
        [flat((2 * z + pz, place(c, py, y), place(c, px, x), c)) for z in range(4) for y in range(2) for x in range(2)]
        for c in range(2)
        for pz, py, px in OFFSETS
    ]


def cubes():
    def along(core, label, cube):
        return 2 * cube + label if core == 0 else (2 * cube + 2 - label) % SIZES[0]

    return [
        [flat((along(c, pz, z), place(c, py, y), place(c, px, x), c)) for pz, py, px in OFFSETS]
        for c in range(2)
        for z in range(SIZES[0] // 2)
        for y in range(2)
        for x in range(2)
    ]


def body(states, episode_end, feature_head, successor_head, horizon_gap, trace_gap):
    steps, width = states.shape[1:]
    num_k = horizon_gap.shape[0]
    kf = successor_head.shape[1]
    nz, ny, nx, nc = SIZES
    swap = [(0, 1), (1, 0)]
    blk = 4 * F
    n = kf // blk
    rows, cols = width // (ny * nx * nc), kf // nz
    half, parts, quads = nz // 2, 4, ny * nx // 4
    tall = parts * quads * rows
    shape = jax.ShapeDtypeStruct
    resid, st, g_local, rates, still_open, coef, features, mask, held, later_head = pl.pallas_call(
        local_kernel,
        in_specs=[HBM] * 6,
        out_specs=[VMEM] * 10,
        out_shape=[
            shape((steps, kf // 2 + F + tall + F), bf16),
            shape((tall, steps), bf16),
            shape((steps, kf // 2), f32),
            shape((num_k + 8, F), f32),
            shape((steps, F), f32),
            shape((2 * num_k, F), f32),
            shape((steps, F), f32),
            shape((steps, steps), bf16),
            shape((steps, width), bf16),
            shape((width, kf // 2), bf16),
        ],
        scratch_shapes=[
            pltpu.SMEM((num_k,), f32),
            pltpu.SMEM((num_k,), f32),
            pltpu.VMEM((1, steps), jnp.int32),
            pltpu.VMEM((width, F), bf16),
            pltpu.VMEM((n // 2, width, blk), bf16),
            pltpu.SemaphoreType.DMA((6 + n // 2,)),
        ],
        compiler_params=params(40),
        name="local",
    )(*[
        pltpu.with_memory_space_constraint(array, pltpu.HBM)
        for array in (horizon_gap, trace_gap, episode_end, states[0], feature_head, successor_head)
    ])
    resid_other = lax.ppermute(resid, "c", swap)
    resid_late, g_late = pl.pallas_call(
        rest_kernel,
        in_specs=[VMEM] * 6,
        out_specs=[VMEM] * 2,
        out_shape=[shape((steps, kf // 2 + F), bf16), shape((steps, kf // 2), f32)],
        compiler_params=params(16),
        cost_estimate=pl.CostEstimate(flops=2 * steps * width * kf, bytes_accessed=6 * MIB, transcendentals=0),
        name="rest",
    )(held, later_head, features, mask, rates, coef)
    resid_late_other = lax.ppermute(resid_late, "c", swap)
    deep = half * quads * rows + 32
    early, st_other, factors = pl.pallas_call(
        functools.partial(early_kernel, num_k),
        in_specs=[VMEM] * 3,
        out_specs=[VMEM] * 3,
        out_shape=[shape((nz // 2, tall, cols), bf16), shape((tall, steps), bf16), shape((F, tall), f32)],
        compiler_params=params(12),
        cost_estimate=pl.CostEstimate(flops=2 * tall * steps * kf, bytes_accessed=4 * MIB, transcendentals=0),
        name="early",
    )(st, resid, resid_other)
    grad = pl.pallas_call(
        functools.partial(grad_kernel, num_k),
        in_specs=[VMEM] * 8,
        out_specs=VMEM,
        out_shape=shape((2 * parts, deep, cols), bf16),
        compiler_params=params(12),
        name="grad",
    )(st, st_other, resid, resid_other, resid_late, resid_late_other, early, factors)
    grad = lax.all_to_all(grad, AXES, 0, 0, axis_index_groups=cubes())
    grad, partner = pl.pallas_call(
        functools.partial(cube_kernel, half, quads, rows, steps),
        in_specs=[VMEM] * 2,
        out_specs=[VMEM] * 2,
        out_shape=[shape((half * quads, rows + 32, cols), bf16), shape((num_k + 8, F), f32)],
        compiler_params=params(12),
        name="sum_cube",
    )(rates, grad)
    grad = lax.all_to_all(grad, AXES, 0, 0, axis_index_groups=alike())
    norm = float(steps * nz * ny * nx * nc) ** -0.5
    returns, head_grad = pl.pallas_call(
        functools.partial(final_kernel, norm),
        in_specs=[VMEM] * 6,
        out_specs=[HBM] * 2,
        out_shape=[shape((steps, kf), bf16), shape((rows, cols), f32)],
        scratch_shapes=[
            pltpu.VMEM((steps, kf), bf16),
            pltpu.VMEM((rows, cols), f32),
            pltpu.SemaphoreType.DMA((kf // cols + 1,)),
        ],
        compiler_params=params(12),
        name="final",
    )(rates, still_open, g_local, g_late, partner, grad)
    return returns[None], head_grad


def solution(mesh):
    grid = Mesh(mesh.devices.reshape(SIZES), AXES)
    traj = ("y", "x", "c")
    return jax.shard_map(
        body,
        mesh=grid,
        in_specs=(P(traj, "z", None), P(traj, "z"), P(), P(), P(), P()),
        out_specs=(P(traj, "z", None), P(traj, "z")),
        check_vma=False,
    )
```

```python
import functools
import itertools
import jax
import jax.numpy as jnp
from jax import lax
from jax.experimental import pallas as pl
from jax.experimental.pallas import tpu as pltpu
from jax.sharding import Mesh, PartitionSpec as P

F = 128
MIB = 1 << 20
AXES = ("z", "y", "x", "c")
SIZES = (8, 4, 4, 2)
f32, bf16 = jnp.float32, jnp.bfloat16
SMEM = pl.BlockSpec(memory_space=pltpu.SMEM)
VMEM = pl.BlockSpec(memory_space=pltpu.VMEM)
HBM = pl.BlockSpec(memory_space=pltpu.HBM)
OFFSETS = list(itertools.product((0, 1), repeat=3))


def iota(shape, dim):
    return lax.broadcasted_iota(jnp.int32, shape, dim)


def coefficients(hg_ref, tg_ref, k):
    hg = jnp.full((1, F), hg_ref[k], f32)
    tg = jnp.full((1, F), tg_ref[k], f32)
    discount = 1.0 - hg
    rate = discount * (1.0 - tg)
    return jnp.log(rate), jnp.sqrt(1.0 - rate * rate), discount * tg / rate


def powers(log_rate, steps):
    a = jnp.exp(iota((steps // 8, F), 0).astype(f32) * (8.0 * log_rate))
    b = jnp.exp(iota((8, F), 0).astype(f32) * log_rate)
    return (a[:, None, :] * b[None, :, :]).reshape(steps, F)


def ends_before(ended_row, steps):
    ended = jnp.broadcast_to(ended_row, (F, steps)).astype(bf16)
    below = (iota((steps, steps), 1) < iota((steps, steps), 0)).astype(f32).astype(bf16)
    return lax.dot_general(below, ended, (((1,), (1,)), ((), ())), preferred_element_type=f32)


def place_in_cube(i, core):
    gray, half = (i ^ (i >> 1)) & 1, i >> 1
    return (gray, half) if core == 0 else (half, gray)


def scan_block(first, top, pred, f, mask, rate_ref, coef_ref, r_ref, g_ref):
    steps = pred.shape[0]
    per, num_k = pred.shape[1] // F, coef_ref.shape[0] // 2
    scaled, backs, biased, carries = [], [], [], []
    for j in range(per):
        k = first + j
        log_rate, scale = rate_ref[k : k + 1, :], coef_ref[k : k + 1, :]
        p = pred[:, j * F : (j + 1) * F].astype(f32)
        biased.append((p, coef_ref[num_k + k : num_k + k + 1, :] * p))
        scaled.append(powers(log_rate, steps) * (scale * f + biased[j][1]))
        backs.append(powers(-log_rate, steps))
    scaled = jnp.concatenate(scaled, axis=1)
    high = scaled.astype(bf16)
    low = (scaled - high.astype(f32)).astype(bf16)
    sums = jnp.dot(mask, high, preferred_element_type=f32)
    sums = sums + jnp.dot(mask, low, preferred_element_type=f32)
    for j in range(per):
        cols = slice((first - top + j) * F, (first - top + j + 1) * F)
        h = backs[j] * sums[:, j * F : (j + 1) * F]
        g = h - biased[j][1]
        g_ref[:, cols] = g
        r_ref[:, cols] = (biased[j][0] - g).astype(bf16)
        carries.append(h[:1])
    return carries


def local_kernel(hg_hbm, tg_hbm, end_hbm, s_hbm, wf_hbm, w_hbm, r_ref, st_ref, g_ref, rate_ref, open_ref, coef_ref,
                 f_ref, mask_ref, s_ref, wl_ref, hg_ref, tg_ref, end_ref, wf_ref, w_ref, sems):
    blocks, _, blk = w_ref.shape
    steps, width = s_ref.shape
    num_k = hg_ref.shape[0]
    half = blocks * blk
    copies = [
        pltpu.make_async_copy(a, b, sems.at[n])
        for n, (a, b) in enumerate(
            [(hg_hbm, hg_ref), (tg_hbm, tg_ref), (end_hbm, end_ref), (s_hbm, s_ref), (wf_hbm, wf_ref)]
            + [(w_hbm.at[:, i * blk : (i + 1) * blk], w_ref.at[i]) for i in range(blocks)]
            + [(w_hbm.at[:, half:], wl_ref)]
        )
    ]
    for copy in copies:
        copy.start()
    for copy in copies[:3]:
        copy.wait()
    ended_row = end_ref[...].astype(f32)
    rows, cols = iota((steps, steps), 0), iota((steps, steps), 1)
    at_row = ends_before(ended_row, steps)
    ended = jnp.broadcast_to(ended_row, (steps, steps)).astype(bf16)
    above = (rows < cols).astype(f32).astype(bf16)
    at_col = jnp.dot(ended, above, preferred_element_type=f32)
    at_rows = jnp.concatenate([at_row] * (steps // F), axis=1)
    mask = jnp.where((at_rows == at_col) & (cols >= rows), 1.0, 0.0).astype(bf16)
    mask_ref[...] = mask
    total = jnp.sum(ended_row, axis=1, keepdims=True)
    still = jnp.where(at_row == total, 1.0, 0.0)
    open_ref[...] = still
    lane = iota((1, F), 1)
    by_lane = jnp.zeros((1, F), f32)
    for k in range(num_k):
        log_rate, scale, beta = coefficients(hg_ref, tg_ref, k)
        rate_ref[k : k + 1, :] = log_rate
        coef_ref[k : k + 1, :] = scale
        coef_ref[num_k + k : num_k + k + 1, :] = beta
        by_lane = jnp.where(lane % num_k == k, log_rate, by_lane)
    rate_ref[num_k:, :] = jnp.broadcast_to(by_lane, (8, F))
    r_ref[:, half : half + F] = (still * backwards(by_lane, steps)).astype(bf16)

    for copy in copies[3:5]:
        copy.wait()
    s = s_ref[...]
    f = jnp.dot(s, wf_ref[...], preferred_element_type=f32)
    f_ref[...] = f
    st = s.T
    here = lax.axis_index("c")
    tall = st_ref.shape[0] // (SIZES[1] * SIZES[2])
    for n in range(st.shape[0] // tall):
        y, x, core = n // (SIZES[2] * SIZES[3]), n // SIZES[3] % SIZES[2], n % SIZES[3]
        (ly, iy), (lx, ix) = place_in_cube(y, core), place_in_cube(x, core)
        at = (ly * 2 + lx) * 4 + iy * 2 + ix
        part = st[n * tall : (n + 1) * tall, :]

        @pl.when(here == core)
        def _():
            st_ref[at * tall : (at + 1) * tall, :] = part

        @pl.when(here != core)
        def _():
            left, top = half + F + at // (steps // tall) * steps, at % (steps // tall) * tall
            r_ref[top : top + tall, left : left + steps] = part

    def predict(i):
        copies[5 + i].wait()
        return jnp.dot(s, w_ref[i], preferred_element_type=f32).astype(bf16)

    following = predict(0)
    carries = []
    for i in range(blocks):
        pred = following
        if i + 1 < blocks:
            following = predict(i + 1)
        carries += scan_block(i * blk // F, 0, pred, f, mask, rate_ref, coef_ref, r_ref, g_ref)
    last = r_ref.shape[1] - F
    free = jnp.where(total == 0.0, 1.0, 0.0)
    carries += [jnp.zeros((num_k - len(carries), F), f32)]
    r_ref[:num_k, last:] = jnp.concatenate(carries, axis=0).astype(bf16)
    r_ref[num_k:, last:] = jnp.broadcast_to(free, (steps - num_k, F)).astype(bf16)
    copies[-1].wait()


def rest_kernel(s_ref, w_ref, f_ref, mask_ref, rate_ref, coef_ref, r_ref, g_ref):
    num_k = coef_ref.shape[0] // 2
    half = w_ref.shape[1]
    blk = half // 2
    carries = []
    for i in range(2):
        pred = jnp.dot(s_ref[...], w_ref[:, i * blk : (i + 1) * blk], preferred_element_type=f32).astype(bf16)
        first = num_k - half // F
        carries += scan_block(first + i * blk // F, first, pred, f_ref[...], mask_ref[...], rate_ref, coef_ref, r_ref, g_ref)
    carries += [jnp.zeros((num_k - len(carries), F), f32)]
    r_ref[:num_k, half:] = jnp.concatenate(carries, axis=0).astype(bf16)
    r_ref[num_k:, half:] = jnp.zeros((r_ref.shape[0] - num_k, F), bf16)


def backwards(log_rate, steps):
    return jnp.exp(steps * log_rate) * powers(-log_rate, steps)


def own_place(axis):
    here = lax.axis_index(axis)
    return tuple(
        jnp.where(lax.axis_index("c") == 0, a, b) for a, b in zip(place_in_cube(here, 0), place_in_cube(here, 1))
    )


def columns_of(st, sto, r_ref, ro_ref, at):
    g = jnp.dot(st, r_ref[:, at], preferred_element_type=f32)
    return (g + jnp.dot(sto, ro_ref[:, at], preferred_element_type=f32)).astype(bf16)


def early_kernel(num_k, st_ref, r_ref, ro_ref, g_ref, sto_ref, at_ref):
    tall, steps = st_ref.shape
    count, _, cols = g_ref.shape
    half, last = count * cols, r_ref.shape[1] - F
    st = st_ref[...]
    sto = jnp.concatenate([ro_ref[:, n : n + steps] for n in range(half + F, last, steps)], axis=0)
    sto_ref[...] = sto
    lane = iota((tall, F), 1)
    a = jnp.dot(st, r_ref[:, half : half + F], preferred_element_type=f32)
    a = jnp.where(lane < num_k, a, jnp.dot(sto, ro_ref[:, half : half + F], preferred_element_type=f32))
    at_ref[...] = a.T
    for z in range(count):
        g_ref[z] = columns_of(st, sto, r_ref, ro_ref, slice(z * cols, (z + 1) * cols))


def grad_kernel(num_k, st_ref, sto_ref, r_ref, ro_ref, rl_ref, rlo_ref, g_ref, at_ref, out_ref):
    tall, steps = st_ref.shape
    labels, deep, cols = out_ref.shape
    count = g_ref.shape[0]
    parts, per = labels // 2, cols // F
    part = tall // parts
    halves = num_k * F // cols // 2
    st, sto, at = st_ref[...], sto_ref[...], at_ref[...]
    last = r_ref.shape[1] - F
    carries = []
    for first, second in ((r_ref, rl_ref), (ro_ref, rlo_ref)):
        a, b = first[: num_k + 1, last:].astype(f32), second[: num_k // 2, count * cols :].astype(f32)
        carries.append(jnp.concatenate([a[: num_k // 2], b, a[num_k:]], axis=0))
    for z in range(2 * halves):
        at_z = slice((z - count) * cols, (z - count + 1) * cols)
        g = g_ref[z] if z < count else columns_of(st, sto, rl_ref, rlo_ref, at_z)
        for n in range(parts):
            out_ref[z % 2 * parts + n, z // 2 * part : (z // 2 + 1) * part, :] = g[n * part : (n + 1) * part]

    def wide(rows):
        return jnp.concatenate(rows, axis=1)

    for pz in range(2):
        for n in range(parts):
            rows = [
                wide([carries[u][k : k + 1] for k in range((2 * half + pz) * per, (2 * half + pz + 1) * per)])
                for half in range(halves)
                for u in range(2)
            ]
            rows += [
                wide([
                    at[u * num_k + k : u * num_k + k + 1, n * part : (n + 1) * part]
                    for k in range((2 * half + pz) * per, (2 * half + pz + 1) * per)
                ])
                for half in range(halves)
                for u in range(2)
            ]
            rows += [wide([carries[u][num_k : num_k + 1]] * per) for u in range(2)]
            rows.append(jnp.zeros((24 - len(rows), cols), f32))
            rows.append(wide([carries[0][m * 8 : (m + 1) * 8] for m in range(num_k // 8)]))
            out_ref[pz * parts + n, halves * part :, :] = jnp.concatenate(rows, axis=0).astype(bf16)


def cube_kernel(halves, quads, rows, steps, rate_ref, in_ref, out_ref, partner_ref):
    part = quads * rows
    num_k = rate_ref.shape[0] - 8
    extra = in_ref[:, halves * part :, :].astype(f32)
    sources = range(in_ref.shape[0])

    def all_of(first):
        return jnp.concatenate([extra[n, first : first + 2] for n in sources], axis=0)

    def own(n):
        block = in_ref[n, halves * part :, :].astype(f32)
        return jnp.concatenate([block[24:, m * F : (m + 1) * F] for m in range(num_k // 8)], axis=0), block[16:17, :F]

    z, core = lax.axis_index("z"), lax.axis_index("c")
    label = z % 2 * 4 + own_place("y")[0] * 2 + own_place("x")[0]
    (mine, my_free), (other, other_free) = own(label), own(label ^ 4)
    partner_ref[:num_k, :] = other
    partner_ref[num_k:, :] = jnp.broadcast_to(other_free, (8, F))
    first = z % 2 == core
    through = jnp.exp(steps * rate_ref[:num_k, :])
    early, late = jnp.where(first, mine, other), jnp.where(first, other, mine)
    joined = early + through * jnp.where(first, my_free, other_free) * late
    apart = (core == 1) & ((z == 0) | (z == SIZES[0] - 1))
    joined = jnp.where(apart, early, joined)
    both = jnp.broadcast_to(my_free * other_free, (num_k, F))

    free = all_of(4 * halves)
    count = free.shape[0] // 2

    def in_time(x):
        return jnp.where(core == 0, x[:count], x[count:]), jnp.where(core == 0, x[count:], x[:count])

    free_early, free_late = in_time(free)
    per = in_ref.shape[2] // F
    for half in range(halves):
        k = [rate_ref[pl.ds((2 * half + z % 2) * per + j, 1), :] for j in range(per)]
        through_k = jnp.exp(steps * jnp.concatenate(k, axis=1))
        (early, late), (at_early, at_late) = in_time(all_of(2 * half)), in_time(all_of(2 * halves + 2 * half))
        inside = jnp.where(apart, 0.0, late).astype(bf16)
        carries = jnp.where(apart, early, early + through_k * free_early * late)
        at = jnp.where(apart, at_late, at_late + through_k * free_late * at_early)
        at_early = at_early.astype(bf16)
        of_k = [
            lax.dot_general(
                at_early[:, j * F : (j + 1) * F],
                inside[:, j * F : (j + 1) * F],
                (((0,), (0,)), ((), ())),
                preferred_element_type=f32,
            )
            for j in range(per)
        ]
        total = jnp.sum(in_ref[:, half * part : (half + 1) * part, :].astype(f32), axis=0)
        total = (total - jnp.concatenate(of_k, axis=1)).astype(bf16)
        for quad in range(quads):
            here = slice(quad * rows, (quad + 1) * rows)
            beside = [at[:, j * F + quad * rows : j * F + (quad + 1) * rows] for j in range(per)]
            beside += [(free_early * free_late)[:, :rows], both[:count, :rows], joined[:count]]
            rest = [joined[count:], jnp.zeros((num_k - count, F), f32)]
            beside = [carries, jnp.concatenate(beside, axis=1), jnp.concatenate(rest, axis=1)]
            out_ref[half * quads + quad, :rows, :] = total[here]
            out_ref[half * quads + quad, rows:, :] = jnp.concatenate(beside, axis=0).astype(bf16)


def final_kernel(norm, rate_ref, open_ref, g_ref, gl_ref, partner_ref, x_ref, out_hbm, y_hbm, out_ref, y_ref, sems):
    rows, cols = y_ref.shape
    per = cols // F
    steps, kf = out_ref.shape
    num_k = rate_ref.shape[0] - 8
    nz, places = SIZES[0], x_ref.shape[0] // (SIZES[0] // 2)
    z_here, core = lax.axis_index("z"), lax.axis_index("c")
    pz = z_here % 2
    (_, iy), (_, ix) = own_place("y"), own_place("x")

    def pair(n):
        block = x_ref[n * places + iy * 2 + ix, rows:, :].astype(f32)
        return jnp.concatenate([block[8:16, F:], block[16:, :F]], axis=0), block[8:9, F - 32 : F - 31]

    through = jnp.exp(steps * rate_ref[:num_k, :])
    later = jnp.where((core == 1) & (pz == 0), pair(0)[0], 0.0)
    for n in range(nz // 2 - 1, 0, -1):
        carry, free = pair(n)
        later = jnp.where(n > z_here // 2, carry + through * through * free * later, later)
    after = partner_ref[:num_k, :] + through * partner_ref[num_k : num_k + 1, :] * later
    h = jnp.where((pz == core) & (z_here < nz - 1), after, later)
    still = open_ref[...]
    copies = []
    for k in range(num_k):
        at = slice(k * F, (k + 1) * F)
        decay = still * backwards(rate_ref[k : k + 1, :], steps)
        g = g_ref[:, at] if k < num_k // 2 else gl_ref[:, (k - num_k // 2) * F : (k - num_k // 2 + 1) * F]
        out_ref[:, at] = (g + decay * h[k : k + 1, :]).astype(bf16)
        if k % per == per - 1:
            at = slice((k + 1 - per) * F, (k + 1) * F)
            copies.append(pltpu.make_async_copy(out_ref.at[:, at], out_hbm.at[:, at], sems.at[len(copies)]))
            copies[-1].start()

    def units(n):
        blocks = [x_ref[n * places + p, rows:, :].astype(f32) for p in range(places)]
        return [jnp.concatenate([block[top : top + 8] for block in blocks], axis=0) for top in (0, 8)]

    k = [rate_ref[pl.ds(z_here * per + j, 1), :] for j in range(per)]
    through = jnp.exp(2 * steps * jnp.concatenate(k, axis=1))
    order = [(2, 1, 0, 3)[i] for i in range(nz // 2)]
    order = [jnp.where(core == 0, 3 - i, (n + 1 - pz) % (nz // 2)) for i, n in enumerate(order)]
    later = jnp.where(core == 0, 0.0, units(order[-1])[0])
    h, at = [], []
    for n in order:
        carry, beside = units(n)
        h.append(later)
        at.append(beside[:, :F])
        later = carry + through * beside[:, per * rows : per * rows + 1] * later
    h = jnp.concatenate(h, axis=0).astype(bf16)
    at = jnp.concatenate(at, axis=0).astype(bf16)
    part = lax.dot_general(at, h, (((0,), (0,)), ((), ())), preferred_element_type=f32)
    part = jnp.concatenate([part[j * rows : (j + 1) * rows, j * F : (j + 1) * F] for j in range(per)], axis=1)
    total = jnp.sum(x_ref[:, :rows, :].astype(f32), axis=0)
    y_ref[...] = (total - part) * norm
    copies.append(pltpu.make_async_copy(y_ref, y_hbm, sems.at[len(copies)]))
    copies[-1].start()
    for copy in copies:
        copy.wait()


def whole(shape):
    return pl.BlockSpec(shape, lambda i: (0,) * len(shape))


def params(mib):
    return pltpu.CompilerParams(vmem_limit_bytes=mib * MIB)


def flat(place):
    n = 0
    for i, size in zip(place, SIZES):
        n = n * size + i
    return n


def place(core, label, index):
    if core == 0:
        return 3 - label if index else label
    return 3 - index if label else index


def alike():
    return [
        [flat((2 * z + pz, place(c, py, y), place(c, px, x), c)) for z in range(4) for y in range(2) for x in range(2)]
        for c in range(2)
        for pz, py, px in OFFSETS
    ]


def cubes():
    def along(core, label, cube):
        return 2 * cube + label if core == 0 else (2 * cube + 2 - label) % SIZES[0]

    return [
        [flat((along(c, pz, z), place(c, py, y), place(c, px, x), c)) for pz, py, px in OFFSETS]
        for c in range(2)
        for z in range(SIZES[0] // 2)
        for y in range(2)
        for x in range(2)
    ]


def body(states, episode_end, feature_head, successor_head, horizon_gap, trace_gap):
    steps, width = states.shape[1:]
    num_k = horizon_gap.shape[0]
    kf = successor_head.shape[1]
    nz, ny, nx, nc = SIZES
    swap = [(0, 1), (1, 0)]
    blk = 4 * F
    n = kf // blk
    rows, cols = width // (ny * nx * nc), kf // nz
    half, parts, quads = nz // 2, 4, ny * nx // 4
    tall = parts * quads * rows
    shape = jax.ShapeDtypeStruct
    resid, st, g_local, rates, still_open, coef, features, mask, held, later_head = pl.pallas_call(
        local_kernel,
        in_specs=[HBM] * 6,
        out_specs=[VMEM] * 10,
        out_shape=[
            shape((steps, kf // 2 + F + tall + F), bf16),
            shape((tall, steps), bf16),
            shape((steps, kf // 2), f32),
            shape((num_k + 8, F), f32),
            shape((steps, F), f32),
            shape((2 * num_k, F), f32),
            shape((steps, F), f32),
            shape((steps, steps), bf16),
            shape((steps, width), bf16),
            shape((width, kf // 2), bf16),
        ],
        scratch_shapes=[
            pltpu.SMEM((num_k,), f32),
            pltpu.SMEM((num_k,), f32),
            pltpu.VMEM((1, steps), jnp.int32),
            pltpu.VMEM((width, F), bf16),
            pltpu.VMEM((n // 2, width, blk), bf16),
            pltpu.SemaphoreType.DMA((6 + n // 2,)),
        ],
        compiler_params=params(40),
        name="local",
    )(*[
        pltpu.with_memory_space_constraint(array, pltpu.HBM)
        for array in (horizon_gap, trace_gap, episode_end, states[0], feature_head, successor_head)
    ])
    resid_other = lax.ppermute(resid, "c", swap)
    resid_late, g_late = pl.pallas_call(
        rest_kernel,
        in_specs=[VMEM] * 6,
        out_specs=[VMEM] * 2,
        out_shape=[shape((steps, kf // 2 + F), bf16), shape((steps, kf // 2), f32)],
        compiler_params=params(16),
        cost_estimate=pl.CostEstimate(flops=2 * steps * width * kf, bytes_accessed=6 * MIB, transcendentals=0),
        name="rest",
    )(held, later_head, features, mask, rates, coef)
    resid_late_other = lax.ppermute(resid_late, "c", swap)
    deep = half * quads * rows + 32
    early, st_other, factors = pl.pallas_call(
        functools.partial(early_kernel, num_k),
        in_specs=[VMEM] * 3,
        out_specs=[VMEM] * 3,
        out_shape=[shape((nz // 2, tall, cols), bf16), shape((tall, steps), bf16), shape((F, tall), f32)],
        compiler_params=params(12),
        cost_estimate=pl.CostEstimate(flops=2 * tall * steps * kf, bytes_accessed=4 * MIB, transcendentals=0),
        name="early",
    )(st, resid, resid_other)
    grad = pl.pallas_call(
        functools.partial(grad_kernel, num_k),
        in_specs=[VMEM] * 8,
        out_specs=VMEM,
        out_shape=shape((2 * parts, deep, cols), bf16),
        compiler_params=params(12),
        name="grad",
    )(st, st_other, resid, resid_other, resid_late, resid_late_other, early, factors)
    grad = lax.all_to_all(grad, AXES, 0, 0, axis_index_groups=cubes())
    grad, partner = pl.pallas_call(
        functools.partial(cube_kernel, half, quads, rows, steps),
        in_specs=[VMEM] * 2,
        out_specs=[VMEM] * 2,
        out_shape=[shape((half * quads, rows + 24, cols), bf16), shape((num_k + 8, F), f32)],
        compiler_params=params(12),
        name="sum_cube",
    )(rates, grad)
    grad = lax.all_to_all(grad, AXES, 0, 0, axis_index_groups=alike())
    norm = float(steps * nz * ny * nx * nc) ** -0.5
    returns, head_grad = pl.pallas_call(
        functools.partial(final_kernel, norm),
        in_specs=[VMEM] * 6,
        out_specs=[HBM] * 2,
        out_shape=[shape((steps, kf), bf16), shape((rows, cols), f32)],
        scratch_shapes=[
            pltpu.VMEM((steps, kf), bf16),
            pltpu.VMEM((rows, cols), f32),
            pltpu.SemaphoreType.DMA((kf // cols + 1,)),
        ],
        compiler_params=params(12),
        name="final",
    )(rates, still_open, g_local, g_late, partner, grad)
    return returns[None], head_grad


def solution(mesh):
    grid = Mesh(mesh.devices.reshape(SIZES), AXES)
    traj = ("y", "x", "c")
    return jax.shard_map(
        body,
        mesh=grid,
        in_specs=(P(traj, "z", None), P(traj, "z"), P(), P(), P(), P()),
        out_specs=(P(traj, "z", None), P(traj, "z")),
        check_vma=False,
    )
```
